128 devices in a mesh: row: 8 (over x, core), col: 16 (over z, y).
Axes of the slice: x: 4, y: 4, z: 4, core: 2. Of those that a mesh axis runs over, the one named last changes fastest.
Arguments:
- object_field: float32 [2, 4096, 8192], P(None, 'row', 'col'), may hold values from -11 to 11
- probe_modes: float32 [2, 2, 256, 256], replicated, may hold values from -4 to 4
- intensities: float32 [256, 256, 256], P(('row', 'col')), may hold values from 0.05 to 5
- positions: int32 [256, 2], replicated, may hold values from 0 to 8191, as said below
- counts: int32 [128], replicated, may hold values from 1 to 2, as said below
Outputs:
- new_object: float32 [2, 4096, 8192], P(None, 'row', 'col')
- new_probe: float32 [2, 2, 256, 256], replicated
The draws below stay inside these ranges and needn't reach their ends.
Inputs may be any that keep to these rules, and one draw needn't show every extreme that they name: Device d (devices numbered row by row over the mesh) holds its counts[d] patterns in its first counts[d] slots, slots d * 2 onward; its other slots are empty. Some device is full in every draw. `positions`: slot s belongs to device d = s div 2, in mesh row r and column c; its patch's top-left pixel lies in that device's tile, rows r * 512 to (r + 1) * 512 - 1 and columns c * 512 to (c + 1) * 512 - 1. In every draw some live slot sits at its tile's last row and last column.
All inputs are finite; a program needn't handle non-finite values.
Results may differ from the reference program's by a relative error of at most 0.00011.
Values sent between devices are 32-bit elements; how exact they have to be, the bound alone decides.
A program may use at most 192 MiB of HBM per device.

```python
import math
import jax
import jax.numpy as jnp
from jax import lax

M = 256
MODES = 2
TY = 512
TX = 512
CAP = 2
ITERS = 3
NY = 4096
NX = 8192
SLOTS = 256


def draw_positions(key, part):
    key = jax.random.fold_in(key, 11)
    key_row, key_col, key_pick = jax.random.split(key, 3)
    column_tiles = NX // TX
    device_total = SLOTS // CAP
    slot_index = jnp.arange(SLOTS, dtype=jnp.int32)
    device_index = slot_index // CAP
    tile_row = device_index // column_tiles
    tile_col = device_index % column_tiles
    local_row = jax.random.randint(key_row, (SLOTS,), 0, TY, dtype=jnp.int32)
    local_col = jax.random.randint(key_col, (SLOTS,), 0, TX, dtype=jnp.int32)
    first_corner = slot_index == 1
    local_row = jnp.where(first_corner, 0, local_row)
    local_col = jnp.where(first_corner, 0, local_col)
    chosen = jax.random.randint(key_pick, (), 0, device_total, dtype=jnp.int32) * CAP
    is_chosen = (slot_index == chosen) | (slot_index == (device_total - 1) * CAP)
    local_row = jnp.where(is_chosen, TY - 1, local_row)
    local_col = jnp.where(is_chosen, TX - 1, local_col)
    return jnp.stack([tile_row * TY + local_row, tile_col * TX + local_col], axis=1).astype(jnp.int32)


def draw_counts(key, part):
    key = jax.random.fold_in(key, 23)
    key_few, key_more, key_pick = jax.random.split(key, 3)
    device_total = SLOTS // CAP
    few_flags = jax.random.randint(key_few, (device_total,), 0, 2, dtype=jnp.int32)
    more_counts = jax.random.randint(key_more, (device_total,), 2, CAP + 1, dtype=jnp.int32)
    counts_now = jnp.where(few_flags == 0, 1, more_counts)
    chosen = jax.random.randint(key_pick, (), 0, device_total, dtype=jnp.int32)
    counts_now = jnp.where(jnp.arange(device_total, dtype=jnp.int32) == chosen, CAP, counts_now)
    return counts_now.astype(jnp.int32)


def draw_object_field(key, part):
    key = jax.random.fold_in(key, 37)
    key_base = jax.random.fold_in(key, 0)
    row_place = jnp.arange(NY, dtype=jnp.float32)[:, None] / NY
    col_place = jnp.arange(NX, dtype=jnp.float32)[None, :] / NX
    base_values = 0.7 * jnp.clip(jax.random.normal(key_base, (2, NY, NX), jnp.float32), -4.0, 4.0)
    trend_scale = 3.0 ** (0.25 * (row_place + col_place))
    return (base_values * trend_scale[None]).astype(jnp.float32)


def shard_levels(own_key, shape, pieces, smallest, high):
    gain = 1.0
    for position, shards_of in pieces:
        draws = jax.random.uniform(jax.random.fold_in(jax.random.fold_in(own_key, 6), position), (shards_of,), jnp.float32, smallest / len(pieces), high / len(pieces))
        gain = gain * jnp.repeat(jnp.exp(draws), shape[position] // shards_of).reshape((-1,) + (1,) * (len(shape) - 1 - position))
    return gain


def scatter_about(key, dims, scale, limit, held_as=jnp.bfloat16):
    return jnp.clip(scale * jax.random.normal(key, dims, jnp.float32), -limit, limit).astype(held_as)


def setup_inputs(seed: int = 0) -> dict:
    streams_of = jax.random.split(jax.random.key(seed), 6)
    return {
        "object_field": draw_object_field(jax.random.fold_in(streams_of[5], 71), 0),
        "probe_modes": scatter_about(streams_of[1], (2, MODES, M, M), 0.7, 4.0, jnp.float32),
        "intensities": jnp.clip(jnp.exp(math.log(5.0) - 4.6051702 * jax.random.uniform(streams_of[2], (SLOTS, M, M), jnp.float32) ** shard_levels(streams_of[2], (SLOTS, M, M), ((0, 128),), -0.2, 0.2)), 0.05, 5.0),
        "positions": draw_positions(jax.random.fold_in(streams_of[5], 71), 0),
        "counts": draw_counts(jax.random.fold_in(streams_of[5], 71), 0),
    }


model_floor = 0.5
damping_share = 0.2
small_term = 1e-06

def reference(object_field, probe_modes, intensities, positions, counts):
    slot_index = jnp.arange(SLOTS, dtype=jnp.int32)
    live_flags = (slot_index % CAP < counts[slot_index // CAP]).astype(jnp.float32)
    zero_index = jnp.zeros((), jnp.int32)
    current_object = object_field
    current_probe = probe_modes
    for sweep_index in range(ITERS):
        probe_complex = current_probe[0] + 1j * current_probe[1]
        probe_power = lax.optimization_barrier(jnp.sum(current_probe[0] ** 2 + current_probe[1] ** 2, axis=0))
        reg_object = damping_share * jnp.mean(probe_power) + small_term
        padded = jnp.pad(current_object, ((0, 0), (0, M), (0, M)))

        def visit_slot(state_now, slot_now):
            accumulated, probe_total, patch_total = state_now
            corner_row = positions[slot_now, 0]
            corner_col = positions[slot_now, 1]
            weight_now = live_flags[slot_now]
            patch_now = lax.dynamic_slice(padded, (zero_index, corner_row, corner_col), (2, M, M))
            patch_complex = patch_now[0] + 1j * patch_now[1]
            exit_wave = probe_complex * patch_complex[None]
            far_field = jnp.fft.fft2(exit_wave, norm='ortho')
            model_power = lax.optimization_barrier(jnp.sum(jnp.real(far_field) ** 2 + jnp.imag(far_field) ** 2, axis=0))
            factor_now = jnp.sqrt(intensities[slot_now] / jnp.maximum(model_power, model_floor))
            change = jnp.fft.ifft2(far_field * factor_now[None], norm='ortho') - exit_wave
            object_term = lax.optimization_barrier(jnp.sum(jnp.conj(probe_complex) * change, axis=0))
            placed = jnp.stack([jnp.real(object_term), jnp.imag(object_term), probe_power]) * weight_now
            window_old = lax.dynamic_slice(accumulated, (zero_index, corner_row, corner_col), (3, M, M))
            accumulated = lax.dynamic_update_slice(accumulated, window_old + placed, (zero_index, corner_row, corner_col))
            probe_term = jnp.conj(patch_complex)[None] * change
            probe_total = probe_total + weight_now * jnp.stack([jnp.real(probe_term), jnp.imag(probe_term)])
            patch_total = patch_total + weight_now * (patch_now[0] ** 2 + patch_now[1] ** 2)
            return ((accumulated, probe_total, patch_total), None)
        start_state = (jnp.zeros((3, NY + M, NX + M), jnp.float32), jnp.zeros((2, MODES, M, M), jnp.float32), jnp.zeros((M, M), jnp.float32))
        final_state, unused = lax.scan(visit_slot, start_state, slot_index)
        accumulated, probe_total, patch_total = final_state
        object_step = accumulated[:, :NY, :NX]
        reg_probe = damping_share * jnp.mean(patch_total) + small_term
        current_object = current_object + object_step[:2] / (object_step[2] + reg_object)
        current_probe = current_probe + probe_total / (patch_total + reg_probe)
    return (current_object, current_probe)
```

```python
import functools
import math

import jax
import jax.numpy as jnp
import ml_dtypes
import numpy as np
from jax import lax
from jax.experimental import pallas as pl
from jax.experimental.pallas import tpu as pltpu
from jax.sharding import PartitionSpec as P

ITERS = 3
M = 256
H = 128
T = 512
MODEL_FLOOR = 0.5
DAMPING = 0.2
SMALL = 1e-06
MESH = pl.DeviceIdType.MESH
F32 = jnp.float32
BF16 = jnp.bfloat16


def tables():
    k = np.arange(H)
    angle = 2.0 * np.pi * ((k[:, None] * k[None, :]) % H) / H
    c, s = np.cos(angle) / 16.0, np.sin(angle) / 16.0

    def three(matrix, axis):
        wide = matrix.astype(np.float32)
        hi = wide.astype(ml_dtypes.bfloat16)
        lo = (wide - hi.astype(np.float32)).astype(ml_dtypes.bfloat16)
        return np.concatenate([hi, hi, lo], axis=axis)

    left = np.block([[c, s], [-s, c]])
    left_back = np.block([[c, -s], [s, c]])
    turn = 2.0 * np.pi * k / M
    rows = np.stack([np.cos(turn), np.sin(turn)])[:, :, None] * np.ones((1, 1, H))
    cols = rows.transpose(0, 2, 1)[:, :16]
    order = np.concatenate([np.arange(0, M, 2), np.arange(1, M, 2)])
    pick = np.zeros((M, M), np.float32)
    pick[np.arange(M), order] = 1.0
    return (
        three(left, 1),
        three(left_back, 1),
        three(left.T, 0),
        three(left_back.T, 0),
        rows.astype(np.float32),
        cols.astype(np.float32),
        pick.astype(ml_dtypes.bfloat16),
        np.ascontiguousarray(pick.T).astype(ml_dtypes.bfloat16),
    )


def dot(a, b):
    return jnp.dot(a, b, preferred_element_type=F32)


def cat(parts, axis):
    return jnp.concatenate(parts, axis=axis)


def split(x):
    hi = x.astype(BF16)
    lo = (x - hi.astype(F32)).astype(BF16)
    return hi, lo


def store_parts(ref, k, row, lane, axis, x):
    hi, lo = split(x)
    for n, part in enumerate((hi, lo, hi)):
        r, c = (row + n * M, lane) if axis == 0 else (row, lane + n * M)
        ref[k, r:r + 16, c:c + H] = part


class Stream:
    def __init__(self, rows, axes, sizes):
        self.half = rows // 2
        self.axes = axes
        self.n = [sizes[a] for a in axes]
        self.r1 = self.half // self.n[0]
        self.r2 = self.r1 // self.n[1]

    def scratch(self):
        vm = lambda *shape: pltpu.VMEM(shape, F32)
        n1, n2, n3 = self.n
        return [
            vm(2, self.half, H),
            vm(ITERS, self.half, H),
            vm(self.half, H),
            vm(ITERS, n1, self.r1, H),
            vm(self.r1, H),
            vm(ITERS, n2, self.r2, H),
            vm(self.r2, H),
            vm(ITERS, n3, self.r2, H),
            vm(ITERS, self.r1, H),
            vm(ITERS, self.half, H),
            vm(ITERS, 2, self.half, H),
            pltpu.SemaphoreType.DMA((ITERS, 7, 4)),
            pltpu.SemaphoreType.DMA((ITERS, 7, 4)),
        ]


def kernel(
    rows_n, cols_n, nz, ny, streams,
    pos, counts, obj_in, probe_in, meas_in, wl_in, wlb_in, wr_in, wrb_in, twr_in, twc_in, pick_in,
    pick_t_in, obj_out, probe,
    meas, wl, wlb, wr, wrb, twr, twc, pick, pick_t,
    obj, acc, den, zbuf, cbuf, power, patch, exits, lop, lout, rop, rout, root, upd, out_up,
    hr, hl, vu, vh,
    load_sem, io_sem, hs, hrs, vs, vrs, us, urs, *ar,
):
    nx = rows_n // 2
    row, col = lax.axis_index("row"), lax.axis_index("col")
    core, xi = lax.rem(row, 2), lax.div(row, 2)
    yi, zi = lax.rem(col, ny), lax.div(col, ny)
    me = {"x": xi, "y": yi, "z": zi}
    size = {"x": nx, "y": ny, "z": nz}

    def device(axis, j):
        if axis == "x":
            return (j * 2 + core, col)
        if axis == "y":
            return (row, zi * ny + j)
        return (row, j * ny + yi)

    partner = (row + 1 - 2 * core, col)
    not_left, not_right = col > 0, col < cols_n - 1
    not_top, not_bottom = row > 0, row < rows_n - 1

    loads = []
    for ch in range(2):
        for b in range(4):
            load = pltpu.make_async_copy(
                obj_in.at[ch, :, pl.ds(b * H, H)], obj.at[ch, b, pl.ds(M, T), :], io_sem.at[ch, b]
            )
            load.start()
            loads.append(load)
    later = []
    for i, (src, dst) in enumerate(
        (
            (meas_in, meas), (pick_in, pick), (pick_t_in, pick_t), (probe_in, probe), (wl_in, wl),
            (wlb_in, wlb), (wr_in, wr), (wrb_in, wrb), (twr_in, twr), (twc_in, twc),
        )
    ):
        load = pltpu.make_async_copy(src, dst, load_sem.at[i])
        load.start()
        later.append(load)

    barrier = pltpu.get_barrier_semaphore()

    def greet(who):
        pl.semaphore_signal(barrier, inc=1, device_id=who, device_id_type=MESH)

    greet(partner)
    peers = 1
    for axis in ("z", "y", "x"):
        for d in range(1, size[axis]):
            greet(device(axis, lax.rem(me[axis] + d, size[axis])))
            peers += 1
    pl.when(not_left)(lambda: greet((row, col - 1)))
    pl.when(not_right)(lambda: greet((row, col + 1)))
    pl.when(not_top)(lambda: greet((row - 1, col)))
    pl.when(not_bottom)(lambda: greet((row + 1, col)))

    zbuf[...] = jnp.zeros_like(zbuf)
    cbuf[...] = jnp.zeros_like(cbuf)

    @pl.when(jnp.logical_not(not_left))
    def _():
        hl[...] = jnp.zeros_like(hl)

    @pl.when(jnp.logical_not(not_right))
    def _():
        hr[...] = jnp.zeros_like(hr)

    @pl.when(jnp.logical_not(not_top))
    def _():
        vu[...] = jnp.zeros_like(vu)

    @pl.when(jnp.logical_not(not_bottom))
    def _():
        vh[...] = jnp.zeros_like(vh)

    for load in loads:
        load.wait()
    pl.semaphore_wait(
        barrier,
        peers
        + not_left.astype(jnp.int32) + not_right.astype(jnp.int32)
        + not_top.astype(jnp.int32) + not_bottom.astype(jnp.int32),
    )

    def remote(src, dst, send, recv, who):
        return pltpu.make_async_remote_copy(
            src_ref=src, dst_ref=dst, send_sem=send, recv_sem=recv, device_id=who, device_id_type=MESH
        )

    def to_left(src, turn, ch, q):
        base = M if src is obj else 0
        return remote(
            src.at[ch, pl.ds(0, 2), pl.ds(base + q * H, H), :], hr.at[turn, ch, q],
            hs.at[turn, 0, ch, q], hrs.at[turn, 0, ch, q], (row, col - 1),
        )

    def to_right(turn, ch, q):
        return remote(
            acc.at[ch, pl.ds(4, 2), pl.ds(q * H, H), :], hl.at[turn, ch, q],
            hs.at[turn, 1, ch, q], hrs.at[turn, 1, ch, q], (row, col + 1),
        )

    def down(it, s, ch):
        return remote(
            upd.at[s, ch], vu.at[it, s, ch], us.at[it, s, ch], urs.at[it, s, ch], (row + 1, col)
        )

    def up(turn, s, ch):
        return remote(
            out_up.at[s, ch], vh.at[turn, s, ch], vs.at[turn, s, ch], vrs.at[turn, s, ch],
            (row - 1, col),
        )

    C = 64
    lane = lax.broadcasted_iota(jnp.int32, (C, H), 1)
    line = lax.broadcasted_iota(jnp.int32, (C, H), 0)

    def place_of(dr, dc, s):
        r, c = row + dr, col + dc
        there = (r >= 0) & (r < rows_n) & (c >= 0) & (c < cols_n)
        r, c = jnp.clip(r, 0, rows_n - 1), jnp.clip(c, 0, cols_n - 1)
        dev = r * cols_n + c
        y = jnp.clip(pos[0, dev * 2 + s] - r * T, 0, T - 1)
        x = jnp.clip(pos[1, dev * 2 + s] - c * T, 0, T - 1)
        live = jnp.where(there & (s < counts[dev]), 1.0, 0.0).astype(F32)
        return y, x, live

    def extract(ch, start, x, store):
        q, r = lax.div(x, H), lax.rem(x, H)
        back = lax.rem(H - r, H)
        keep = lane < H - r
        for i in range(0, M, C):
            b = [pltpu.roll(obj[ch, q + j, pl.ds(start + i, C), :], back, 1) for j in range(3)]
            store(i, jnp.where(keep, b[0], b[1]), jnp.where(keep, b[1], b[2]))

    def spread(z, load, x):
        r = lax.rem(x, H)
        keep = lane >= r
        for i in range(0, M, C):
            u0, u1 = load(i)
            a, b = pltpu.roll(u0, r, 1), pltpu.roll(u1, r, 1)
            z[0, T + i:T + i + C, :] = jnp.where(keep, a, 0.0)
            z[1, T + i:T + i + C, :] = jnp.where(keep, b, a)
            z[2, T + i:T + i + C, :] = jnp.where(keep, 0.0, b)

    def add_placed(z, dst, blocks, dr, dc, y, x, weight):
        q = lax.div(x, H) + 4 * dc
        length = T if dr == 0 else M
        start = T - y - dr * T
        if dr != 0:
            start = jnp.minimum(start, 3 * M)
        for b in blocks:
            j = b - q
            inside = jnp.where((j >= 0) & (j <= 2), weight, 0.0).astype(F32)
            near = jnp.clip(j, 0, 2)
            for i in range(0, length, C):
                dst[b, i:i + C, :] += z[near, pl.ds(start + i, C), :] * inside

    def send_up(turn, ch):
        for s in range(2):
            y, x, _ = place_of(-1, 0, s)

            def store(i, b0, b1, s=s):
                out_up[s, ch, 0, i:i + C, :] = b0
                out_up[s, ch, 1, i:i + C, :] = b1

            extract(ch, jnp.maximum(y - T, -M) + M, x, store)
            pl.when(not_top)(lambda: up(turn, s, ch).start())

    first = [(ch, q) for half in range(2) for ch in range(2) for q in (2 * half, 2 * half + 1)]

    def first_piece(n):
        pl.when(not_left)(lambda: to_left(obj, 0, *first[n]).start())

    first_piece(0)
    first_piece(1)

    for load in later:
        load.wait()

    for s in range(2):
        value = meas[s]
        for step in range(2):
            h = value.astype(BF16)
            rest = value - h.astype(F32)
            m = rest.astype(BF16)
            low = (rest - m.astype(F32)).astype(BF16)
            if step == 0:
                value = (dot(pick[...], h) + dot(pick[...], m)) + dot(pick[...], low)
            else:
                value = (dot(h, pick_t[...]) + dot(m, pick_t[...])) + dot(low, pick_t[...])
        root[s] = jnp.sqrt(value)

    for n, (ch, q) in enumerate(first):
        pl.when(not_right)(lambda: to_left(obj, 0, ch, q).wait_recv())
        if n + 2 < len(first):
            first_piece(n + 2)
        for b in range(2):
            for i in range(0, H, C):
                obj[ch, 4 + b, M + q * H + i:M + q * H + i + C, :] = hr[0, ch, q, b, i:i + C, :]
        if q == 1:
            send_up(0, ch)

    def take(it, s):
        y, x, live = place_of(0, 0, s)

        def store(i, b0, b1, ch):
            own = line + i < T - y
            parts = (b0, b1)
            for b in range(2):
                value = jnp.where(own, parts[b], vh[it, s, ch, b, i:i + C, :])
                patch[s, ch, i:i + C, b * H:(b + 1) * H] = value
                sum_ref(2, 0, b)[i:i + C, :] += value * value * live

        for ch in range(2):
            extract(ch, M + y, x, functools.partial(store, ch=ch))

    def slot(it, s):
        _, _, live = place_of(0, 0, s)
        cc, sc = twc[0], twc[1]
        lanes = (slice(0, H), slice(H, M))
        for k in range(2):
            for i in range(0, H, 16):
                cr, sr = twr[0, i:i + 16, :], twr[1, i:i + 16, :]
                for b in range(2):
                    er, ei = [], []
                    for t in (i, i + H):
                        at = (slice(t, t + 16), lanes[b])
                        pr, pi = patch[(s, 0) + at], patch[(s, 1) + at]
                        qr, qi = probe[(0, k) + at], probe[(1, k) + at]
                        er.append(qr * pr - qi * pi)
                        ei.append(qr * pi + qi * pr)
                        exits[(k, 0) + at] = er[-1]
                        exits[(k, 1) + at] = ei[-1]
                    dr, di = er[0] - er[1], ei[0] - ei[1]
                    store_parts(lop, k, i, b * H, 0, er[0] + er[1])
                    store_parts(lop, k, i + H, b * H, 0, ei[0] + ei[1])
                    store_parts(lop, k, i, M + b * H, 0, dr * cr + di * sr)
                    store_parts(lop, k, i + H, M + b * H, 0, di * cr - dr * sr)
            lout[k] = dot(wl[...], lop[k])
        for k in range(2):
            for i in range(0, M, 16):
                j, c = i % H, (i // H) * M
                lr = [lout[k, j:j + 16, c + b * H:c + b * H + H] for b in range(2)]
                li = [lout[k, j + H:j + H + 16, c + b * H:c + b * H + H] for b in range(2)]
                dr, di = lr[0] - lr[1], li[0] - li[1]
                store_parts(rop, k, i, 0, 1, lr[0] + lr[1])
                store_parts(rop, k, i, H, 1, li[0] + li[1])
                store_parts(rop, k, i + M, 0, 1, dr * cc + di * sc)
                store_parts(rop, k, i + M, H, 1, di * cc - dr * sc)
            rout[k] = dot(rop[k], wr[...])
        for i in range(0, 2 * M, 16):
            f = [[rout[k, i:i + 16, lanes[b]] for b in range(2)] for k in range(2)]
            model = (f[0][0] * f[0][0] + f[0][1] * f[0][1]) + (f[1][0] * f[1][0] + f[1][1] * f[1][1])
            scale = root[s, i % M:i % M + 16, lanes[i // M]]
            scale = scale * lax.rsqrt(jnp.maximum(model, MODEL_FLOOR))
            for k in range(2):
                for b in range(2):
                    store_parts(rop, k, i, b * H, 1, f[k][b] * scale)
        for k in range(2):
            rout[k] = dot(rop[k], wrb[...])
        for k in range(2):
            for i in range(0, M, 16):
                er, ei = rout[k, i:i + 16, lanes[0]], rout[k, i:i + 16, lanes[1]]
                dr, di = rout[k, i + M:i + M + 16, lanes[0]], rout[k, i + M:i + M + 16, lanes[1]]
                tr, ti = dr * cc - di * sc, di * cc + dr * sc
                j, c = i % H, (i // H) * M
                store_parts(lop, k, j, c, 0, er + tr)
                store_parts(lop, k, j, c + H, 0, er - tr)
                store_parts(lop, k, j + H, c, 0, ei + ti)
                store_parts(lop, k, j + H, c + H, 0, ei - ti)
            lout[k] = dot(wlb[...], lop[k])
        for i in range(0, H, 16):
            cr, sr = twr[0, i:i + 16, :], twr[1, i:i + 16, :]
            for b in range(2):
                u = [[None, None], [None, None]]
                for k in range(2):
                    c = b * H
                    er, ei = lout[k, i:i + 16, c:c + H], lout[k, i + H:i + H + 16, c:c + H]
                    dr = lout[k, i:i + 16, M + c:M + c + H]
                    di = lout[k, i + H:i + H + 16, M + c:M + c + H]
                    tr, ti = dr * cr - di * sr, di * cr + dr * sr
                    for n, (gr, gi) in enumerate(((er + tr, ei + ti), (er - tr, ei - ti))):
                        t = i + n * H
                        at = (slice(t, t + 16), lanes[b])
                        gr = (gr - exits[(k, 0) + at]) * live
                        gi = (gi - exits[(k, 1) + at]) * live
                        qr, qi = probe[(0, k) + at], probe[(1, k) + at]
                        pr, pi = patch[(s, 0) + at], patch[(s, 1) + at]
                        ur, ui = qr * gr + qi * gi, qr * gi - qi * gr
                        if k == 0:
                            u[n] = [ur, ui]
                        else:
                            upd[s, 0, b, t:t + 16, :] = u[n][0] + ur
                            upd[s, 1, b, t:t + 16, :] = u[n][1] + ui
                        sum_ref(k, 0, b)[t:t + 16, :] += pr * gr + pi * gi
                        sum_ref(k, 1, b)[t:t + 16, :] += pr * gi - pi * gr
        for ch in range(2):
            pl.when(not_bottom)(lambda: down(it, s, ch).start())

    def place(ch, dr, s, src):
        y, x, _ = place_of(dr, 0, s)
        spread(zbuf.at[ch], lambda i: (src[0, i:i + C, :], src[1, i:i + C, :]), x)
        add_placed(zbuf.at[ch], acc.at[ch], range(6), dr, 0, y, x, 1.0)

    def sum_ref(k, part, b):
        if k == 2:
            return ar[26].at[b]
        return ar[13 * k].at[part, pl.ds(b * M, M), :]

    def group(it, n, phase, axis, src, dst):
        ssem, rsem = ar[13 * n + 11], ar[13 * n + 12]
        out = []
        for d in range(1, size[axis]):
            j = lax.rem(me[axis] + d, size[axis])
            out.append(
                remote(src(j), dst, ssem.at[it, phase, d], rsem.at[it, phase, d], device(axis, j))
            )
        return out

    def phase_copies(it, n, phase):
        st = streams[n]
        own, cin, m0, r1, m1, r2, m2, r3, g2, g1, gc, ssem, rsem = ar[13 * n:13 * n + 13]
        a, b, c = st.axes
        R1, R2 = st.r1, st.r2
        rows_of = lambda j, r: pl.ds(pl.multiple_of(j * r, 8), r)
        if phase == 0:
            return [remote(own.at[1 - core], cin.at[it], ssem.at[it, 0, 0], rsem.at[it, 0, 0], partner)]
        if phase == 1:
            return group(it, n, 1, a, lambda j: m0.at[rows_of(j, R1), :], r1.at[it, me[a]])
        if phase == 2:
            return group(it, n, 2, b, lambda j: m1.at[rows_of(j, R2), :], r2.at[it, me[b]])
        if phase == 3:
            return group(it, n, 3, c, lambda j: m2, r3.at[it, me[c]])
        if phase == 4:
            part = g2.at[it, rows_of(me[b], R2), :]
            return group(it, n, 4, b, lambda j: part, part)
        if phase == 5:
            part = g1.at[it, rows_of(me[a], R1), :]
            return group(it, n, 5, a, lambda j: part, part)
        part = gc.at[it, core]
        return [remote(part, part, ssem.at[it, 6, 0], rsem.at[it, 6, 0], partner)]

    def ar_start(it, which):
        for n in which:
            for copy in phase_copies(it, n, 0):
                copy.start()

    def ar_step(it, which, phase):
        for n in which:
            st = streams[n]
            own, cin, m0, r1, m1, r2, m2, r3, g2, g1, gc, ssem, rsem = ar[13 * n:13 * n + 13]
            a, b, c = st.axes
            rows_of = lambda j, r: pl.ds(pl.multiple_of(j * r, 8), r)
            for copy in phase_copies(it, n, phase):
                copy.wait_recv()
            if phase == 0:
                for i in range(0, st.half, C):
                    m0[i:i + C, :] = own[core, i:i + C, :] + cin[it, i:i + C, :]
                r1[it, me[a]] = m0[rows_of(me[a], st.r1), :]
            elif phase == 1:
                m1[...] = functools.reduce(lambda p, q: p + q, [r1[it, j] for j in range(st.n[0])])
                r2[it, me[b]] = m1[rows_of(me[b], st.r2), :]
            elif phase == 2:
                m2[...] = functools.reduce(lambda p, q: p + q, [r2[it, j] for j in range(st.n[1])])
                r3[it, me[c]] = m2[...]
            elif phase == 3:
                g2[it, rows_of(me[b], st.r2), :] = functools.reduce(
                    lambda p, q: p + q, [r3[it, j] for j in range(st.n[2])]
                )
            elif phase == 4:
                g1[it, rows_of(me[a], st.r1), :] = g2[it]
            elif phase == 5:
                gc[it, core] = g1[it]
            if phase < 6:
                for copy in phase_copies(it, n, phase + 1):
                    copy.start()

    mode_sums, power_sum = (0, 1), (2,)

    def iteration(it, _):
        more = it < ITERS - 1
        send_left = not_left & more
        get_right = not_right & more
        acc[...] = jnp.zeros_like(acc)
        for n in range(3):
            ar[13 * n][...] = jnp.zeros_like(ar[13 * n])

        for s in range(2):
            take(it, s)
        ar_start(it, power_sum)

        def one(s, carry):
            slot(it, s)

            @pl.when(s == 0)
            def _():
                ar_step(it, power_sum, 0)

            return carry

        lax.fori_loop(0, 2, one, 0)
        ar_start(it, mode_sums)

        def send(ch, q):
            pl.when(not_right)(lambda: to_right(it, ch, q).start())
            pl.when(send_left)(lambda: to_left(acc, it + 1, ch, q).start())

        def arrive(ch, q):
            pl.when(not_left)(lambda: to_right(it, ch, q).wait_recv())
            pl.when(get_right)(lambda: to_left(acc, it + 1, ch, q).wait_recv())

        def update(ch, q):
            for i in range(q * H, q * H + H, C):
                rows, there, j = slice(i, i + C), slice(M + i, M + i + C), i - q * H
                for b in range(4):
                    step = acc[ch, b, rows, :]
                    if b < 2:
                        step = step + hl[it, ch, q, b, j:j + C, :]
                    obj[ch, b, there, :] += step * den[b, rows, :]

            @pl.when(get_right)
            def _():
                for i in range(q * H, q * H + H, C):
                    rows, there, j = slice(i, i + C), slice(M + i, M + i + C), i - q * H
                    for b in range(2):
                        step = acc[ch, 4 + b, rows, :] + hr[it + 1, ch, q, b, j:j + C, :]
                        obj[ch, 4 + b, there, :] += step * den[4 + b, rows, :]

        def below(s, ch):
            pl.when(not_top)(lambda: down(it, s, ch).wait_recv())
            place(ch, -1, s, vu.at[it, s, ch])

        for ch in range(2):
            for s in range(2):
                place(ch, 0, s, upd.at[s, ch])
            if ch == 0:
                send(0, 2)
                send(0, 3)
        ar_step(it, power_sum, 1)
        ar_step(it, mode_sums, 0)
        for q in range(2):
            if q == 0:
                below(0, 0)
                below(1, 0)
            arrive(0, 2 + q)
            send(0, q)
        below(0, 1)
        below(1, 1)
        ar_step(it, power_sum, 2)

        power_all = jnp.zeros((C, H), F32)
        for b in range(2):
            for i in range(0, M, C):
                at = (slice(i, i + C), slice(b * H, b * H + H))
                square = (
                    probe[(0, 0) + at] ** 2 + probe[(1, 0) + at] ** 2
                    + probe[(0, 1) + at] ** 2 + probe[(1, 1) + at] ** 2
                )
                power[b, i:i + C, :] = square
                power_all = power_all + square
        reg_object = DAMPING * (jnp.sum(power_all) * (1.0 / (M * M))) + SMALL
        den[...] = jnp.zeros_like(den)
        for dr in (0, -1):
            for dc, blocks in ((0, range(6)), (-1, range(2)), (1, range(4, 6))):

                def cover(s, carry, dr=dr, dc=dc, blocks=blocks):
                    y, x, live = place_of(dr, dc, s)
                    spread(cbuf, lambda i: (power[0, i:i + C, :], power[1, i:i + C, :]), x)
                    add_placed(cbuf, den, blocks, dr, dc, y, x, live)
                    return carry

                lax.fori_loop(0, 2, cover, 0)
        for b in range(6):
            for i in range(0, T, C):
                den[b, i:i + C, :] = 1.0 / (den[b, i:i + C, :] + reg_object)

        arrive(0, 0)
        send(1, 0)
        update(0, 0)
        ar_step(it, mode_sums, 1)
        arrive(0, 1)
        send(1, 1)
        update(0, 1)
        pl.when(more)(lambda: send_up(it + 1, 0))
        ar_step(it, power_sum, 3)
        ar_step(it, mode_sums, 2)
        arrive(1, 0)
        send(1, 2)
        update(1, 0)
        ar_step(it, mode_sums, 3)
        arrive(1, 1)
        send(1, 3)
        update(1, 1)
        pl.when(more)(lambda: send_up(it + 1, 1))
        update(0, 2)
        update(0, 3)
        ar_step(it, power_sum, 4)
        ar_step(it, mode_sums, 4)
        arrive(1, 2)
        update(1, 2)
        ar_step(it, power_sum, 5)
        ar_step(it, mode_sums, 5)
        arrive(1, 3)
        update(1, 3)
        for n in range(len(streams)):
            for copy in phase_copies(it, n, 6):
                copy.wait_recv()

        def total(k, part, b, i):
            if k == 2:
                return ar[36][it, b, i:i + C, :]
            return ar[13 * k + 10][it, part, b * M + i:b * M + i + C, :]

        sums = jnp.zeros((C, H), F32)
        for b in range(2):
            for i in range(0, M, C):
                sums = sums + total(2, 0, b, i)
        reg_probe = DAMPING * (jnp.sum(sums) * (1.0 / (M * M))) + SMALL
        for b in range(2):
            for i in range(0, M, C):
                scale = 1.0 / (total(2, 0, b, i) + reg_probe)
                for k in range(2):
                    for part in range(2):
                        at = (part, k, slice(i, i + C), slice(b * H, b * H + H))
                        probe[at] += total(k, part, b, i) * scale

        for n in range(len(streams)):
            for phase in range(7):
                for copy in phase_copies(it, n, phase):
                    copy.wait_send()
        for ch in range(2):
            for q in range(4):
                pl.when(not_right)(lambda: to_right(it, ch, q).wait_send())
                pl.when(send_left)(lambda: to_left(acc, it + 1, ch, q).wait_send())
            for s in range(2):
                pl.when(not_bottom)(lambda: down(it, s, ch).wait_send())
                pl.when(not_bottom & more)(lambda: up(it + 1, s, ch).wait_recv())
                pl.when(not_top & more)(lambda: up(it + 1, s, ch).wait_send())
        return 0

    for ch in range(2):
        for q in range(4):
            pl.when(not_left)(lambda: to_left(obj, 0, ch, q).wait_send())
        for s in range(2):
            pl.when(not_bottom)(lambda: up(0, s, ch).wait_recv())
            pl.when(not_top)(lambda: up(0, s, ch).wait_send())

    lax.fori_loop(0, ITERS, iteration, 0)

    stores = []
    for ch in range(2):
        for b in range(4):
            store = pltpu.make_async_copy(
                obj.at[ch, b, pl.ds(M, T), :], obj_out.at[ch, :, pl.ds(b * H, H)], io_sem.at[ch, b]
            )
            store.start()
            stores.append(store)
    for store in stores:
        store.wait()


def shards(rows_n, cols_n, nz, ny, object_field, probe_modes, intensities, positions, counts):
    sizes = {"x": rows_n // 2, "y": ny, "z": nz}
    streams = (
        Stream(1024, ("x", "z", "y"), sizes),
        Stream(1024, ("x", "y", "z"), sizes),
        Stream(512, ("x", "z", "y"), sizes),
    )
    vm = lambda *shape: pltpu.VMEM(shape, F32)
    sem = lambda *shape: pltpu.SemaphoreType.DMA(shape)
    consts = [jnp.asarray(t) for t in tables()]
    scratch = [vm(2, M, M)] + [pltpu.VMEM(t.shape, t.dtype) for t in consts]
    scratch += [
        vm(2, 6, 1024, H),
        vm(2, 6, T, H),
        vm(6, T, H),
        vm(2, 3, 1024, H),
        vm(3, 1024, H),
        vm(2, M, H),
        vm(2, 2, M, M),
        vm(2, 2, M, M),
        pltpu.VMEM((2, 3 * M, 2 * M), BF16),
        vm(2, M, 2 * M),
        pltpu.VMEM((2, 2 * M, 3 * M), BF16),
        vm(2, 2 * M, M),
        vm(2, M, M),
        vm(2, 2, 2, M, H),
        vm(2, 2, 2, M, H),
        vm(ITERS, 2, 4, 2, H, H),
        vm(ITERS, 2, 4, 2, H, H),
        vm(ITERS, 2, 2, 2, M, H),
        vm(ITERS, 2, 2, 2, M, H),
        sem(10),
        sem(2, 4),
        sem(ITERS, 2, 2, 4),
        sem(ITERS, 2, 2, 4),
        sem(ITERS, 2, 2),
        sem(ITERS, 2, 2),
        sem(ITERS, 2, 2),
        sem(ITERS, 2, 2),
    ]
    for st in streams:
        scratch += st.scratch()
    smem = pl.BlockSpec(memory_space=pltpu.SMEM)
    vmem = pl.BlockSpec(memory_space=pltpu.VMEM)
    hbm = pl.BlockSpec(memory_space=pl.ANY)
    return pl.pallas_call(
        functools.partial(kernel, rows_n, cols_n, nz, ny, streams),
        out_shape=(
            jax.ShapeDtypeStruct((2, T, T), F32),
            jax.ShapeDtypeStruct((2, 2, M, M), F32),
        ),
        in_specs=[smem, smem, hbm, hbm, hbm] + [hbm] * len(consts),
        out_specs=(hbm, vmem),
        scratch_shapes=scratch,
        compiler_params=pltpu.CompilerParams(
            collective_id=0, has_side_effects=True, vmem_limit_bytes=62 * 1024 * 1024
        ),
        name="ptycho",
    )(positions.T, counts, object_field, probe_modes, intensities, *consts)


def solution(mesh):
    rows_n, cols_n = mesh.shape["row"], mesh.shape["col"]
    ny = math.isqrt(cols_n)
    nz = cols_n // ny
    placed = (P(None, "row", "col"), P(), P(("row", "col"), None, None), P(), P())
    return jax.shard_map(
        functools.partial(shards, rows_n, cols_n, nz, ny),
        mesh=mesh,
        in_specs=placed,
        out_specs=(P(None, "row", "col"), P()),
        check_vma=False,
    )
```

```python
import functools
import math

import jax
import jax.numpy as jnp
import ml_dtypes
import numpy as np
from jax import lax
from jax.experimental import pallas as pl
from jax.experimental.pallas import tpu as pltpu
from jax.sharding import PartitionSpec as P

ITERS = 3
M = 256
H = 128
T = 512
MODEL_FLOOR = 0.5
DAMPING = 0.2
SMALL = 1e-06
MESH = pl.DeviceIdType.MESH
F32 = jnp.float32
BF16 = jnp.bfloat16


def tables():
    k = np.arange(H)
    angle = 2.0 * np.pi * ((k[:, None] * k[None, :]) % H) / H
    c, s = np.cos(angle) / 16.0, np.sin(angle) / 16.0

    def three(matrix, axis):
        wide = matrix.astype(np.float32)
        hi = wide.astype(ml_dtypes.bfloat16)
        lo = (wide - hi.astype(np.float32)).astype(ml_dtypes.bfloat16)
        return np.concatenate([hi, hi, lo], axis=axis)

    left = np.block([[c, s], [-s, c]])
    left_back = np.block([[c, -s], [s, c]])
    turn = 2.0 * np.pi * k / M
    rows = np.stack([np.cos(turn), np.sin(turn)])[:, :, None] * np.ones((1, 1, H))
    cols = rows.transpose(0, 2, 1)[:, :16]
    order = np.concatenate([np.arange(0, M, 2), np.arange(1, M, 2)])
    pick = np.zeros((M, M), np.float32)
    pick[np.arange(M), order] = 1.0
    return (
        three(left, 1),
        three(left_back, 1),
        three(left.T, 0),
        three(left_back.T, 0),
        rows.astype(np.float32),
        cols.astype(np.float32),
        pick.astype(ml_dtypes.bfloat16),
        np.ascontiguousarray(pick.T).astype(ml_dtypes.bfloat16),
    )


def dot(a, b):
    return jnp.dot(a, b, preferred_element_type=F32)


def cat(parts, axis):
    return jnp.concatenate(parts, axis=axis)


def split(x):
    hi = x.astype(BF16)
    lo = (x - hi.astype(F32)).astype(BF16)
    return hi, lo


def store_parts(ref, k, row, lane, axis, x):
    hi, lo = split(x)
    for n, part in enumerate((hi, lo, hi)):
        r, c = (row + n * M, lane) if axis == 0 else (row, lane + n * M)
        ref[k, r:r + 16, c:c + H] = part


class Stream:
    def __init__(self, rows, axes, sizes):
        self.half = rows // 2
        self.axes = axes
        self.n = [sizes[a] for a in axes]
        self.r1 = self.half // self.n[0]
        self.r2 = self.r1 // self.n[1]

    def scratch(self):
        vm = lambda *shape: pltpu.VMEM(shape, F32)
        n1, n2, n3 = self.n
        return [
            vm(2, self.half, H),
            vm(ITERS, self.half, H),
            vm(self.half, H),
            vm(ITERS, n1, self.r1, H),
            vm(self.r1, H),
            vm(ITERS, n2, self.r2, H),
            vm(self.r2, H),
            vm(ITERS, n3, self.r2, H),
            vm(ITERS, self.r1, H),
            vm(ITERS, self.half, H),
            vm(ITERS, 2, self.half, H),
            pltpu.SemaphoreType.DMA((ITERS, 7, 4)),
            pltpu.SemaphoreType.DMA((ITERS, 7, 4)),
        ]


def kernel(
    rows_n, cols_n, nz, ny, streams,
    pos, counts, obj_in, probe_in, meas_in, wl_in, wlb_in, wr_in, wrb_in, twr_in, twc_in, pick_in,
    pick_t_in, obj_out, probe,
    meas, wl, wlb, wr, wrb, twr, twc, pick, pick_t,
    obj, acc, den, zbuf, cbuf, power, patch, exits, lop, lout, rop, rout, root, upd, out_up,
    hr, hl, vu, vh,
    load_sem, io_sem, hs, hrs, vs, vrs, us, urs, *ar,
):
    nx = rows_n // 2
    row, col = lax.axis_index("row"), lax.axis_index("col")
    core, xi = lax.rem(row, 2), lax.div(row, 2)
    yi, zi = lax.rem(col, ny), lax.div(col, ny)
    me = {"x": xi, "y": yi, "z": zi}
    size = {"x": nx, "y": ny, "z": nz}

    def device(axis, j):
        if axis == "x":
            return (j * 2 + core, col)
        if axis == "y":
            return (row, zi * ny + j)
        return (row, j * ny + yi)

    partner = (row + 1 - 2 * core, col)
    not_left, not_right = col > 0, col < cols_n - 1
    not_top, not_bottom = row > 0, row < rows_n - 1

    loads = []
    for ch in range(2):
        for b in range(4):
            load = pltpu.make_async_copy(
                obj_in.at[ch, :, pl.ds(b * H, H)], obj.at[ch, b, pl.ds(M, T), :], io_sem.at[ch, b]
            )
            load.start()
            loads.append(load)
    later = []
    for i, (src, dst) in enumerate(
        (
            (meas_in, meas), (pick_in, pick), (pick_t_in, pick_t), (probe_in, probe), (wl_in, wl),
            (wlb_in, wlb), (wr_in, wr), (wrb_in, wrb), (twr_in, twr), (twc_in, twc),
        )
    ):
        load = pltpu.make_async_copy(src, dst, load_sem.at[i])
        load.start()
        later.append(load)

    barrier = pltpu.get_barrier_semaphore()

    def greet(who):
        pl.semaphore_signal(barrier, inc=1, device_id=who, device_id_type=MESH)

    greet(partner)
    peers = 1
    for axis in ("z", "y", "x"):
        for d in range(1, size[axis]):
            greet(device(axis, lax.rem(me[axis] + d, size[axis])))
            peers += 1
    pl.when(not_left)(lambda: greet((row, col - 1)))
    pl.when(not_right)(lambda: greet((row, col + 1)))
    pl.when(not_top)(lambda: greet((row - 1, col)))
    pl.when(not_bottom)(lambda: greet((row + 1, col)))

    zbuf[...] = jnp.zeros_like(zbuf)
    cbuf[...] = jnp.zeros_like(cbuf)

    @pl.when(jnp.logical_not(not_left))
    def _():
        hl[...] = jnp.zeros_like(hl)

    @pl.when(jnp.logical_not(not_right))
    def _():
        hr[...] = jnp.zeros_like(hr)

    @pl.when(jnp.logical_not(not_top))
    def _():
        vu[...] = jnp.zeros_like(vu)

    @pl.when(jnp.logical_not(not_bottom))
    def _():
        vh[...] = jnp.zeros_like(vh)

    for load in loads:
        load.wait()
    pl.semaphore_wait(
        barrier,
        peers
        + not_left.astype(jnp.int32) + not_right.astype(jnp.int32)
        + not_top.astype(jnp.int32) + not_bottom.astype(jnp.int32),
    )

    def remote(src, dst, send, recv, who):
        return pltpu.make_async_remote_copy(
            src_ref=src, dst_ref=dst, send_sem=send, recv_sem=recv, device_id=who, device_id_type=MESH
        )

    def to_left(src, turn, ch, q):
        base = M if src is obj else 0
        return remote(
            src.at[ch, pl.ds(0, 2), pl.ds(base + q * H, H), :], hr.at[turn, ch, q],
            hs.at[turn, 0, ch, q], hrs.at[turn, 0, ch, q], (row, col - 1),
        )

    def to_right(turn, ch, q):
        return remote(
            acc.at[ch, pl.ds(4, 2), pl.ds(q * H, H), :], hl.at[turn, ch, q],
            hs.at[turn, 1, ch, q], hrs.at[turn, 1, ch, q], (row, col + 1),
        )

    def down(it, s, ch):
        return remote(
            upd.at[s, ch], vu.at[it, s, ch], us.at[it, s, ch], urs.at[it, s, ch], (row + 1, col)
        )

    def up(turn, s, ch):
        return remote(
            out_up.at[s, ch], vh.at[turn, s, ch], vs.at[turn, s, ch], vrs.at[turn, s, ch],
            (row - 1, col),
        )

    C = 64
    lane = lax.broadcasted_iota(jnp.int32, (C, H), 1)
    line = lax.broadcasted_iota(jnp.int32, (C, H), 0)

    def place_of(dr, dc, s):
        r, c = row + dr, col + dc
        there = (r >= 0) & (r < rows_n) & (c >= 0) & (c < cols_n)
        r, c = jnp.clip(r, 0, rows_n - 1), jnp.clip(c, 0, cols_n - 1)
        dev = r * cols_n + c
        y = jnp.clip(pos[0, dev * 2 + s] - r * T, 0, T - 1)
        x = jnp.clip(pos[1, dev * 2 + s] - c * T, 0, T - 1)
        live = jnp.where(there & (s < counts[dev]), 1.0, 0.0).astype(F32)
        return y, x, live

    def extract(ch, start, x, store):
        q, r = lax.div(x, H), lax.rem(x, H)
        back = lax.rem(H - r, H)
        keep = lane < H - r
        for i in range(0, M, C):
            b = [pltpu.roll(obj[ch, q + j, pl.ds(start + i, C), :], back, 1) for j in range(3)]
            store(i, jnp.where(keep, b[0], b[1]), jnp.where(keep, b[1], b[2]))

    def spread(z, load, x):
        r = lax.rem(x, H)
        keep = lane >= r
        for i in range(0, M, C):
            u0, u1 = load(i)
            a, b = pltpu.roll(u0, r, 1), pltpu.roll(u1, r, 1)
            z[0, T + i:T + i + C, :] = jnp.where(keep, a, 0.0)
            z[1, T + i:T + i + C, :] = jnp.where(keep, b, a)
            z[2, T + i:T + i + C, :] = jnp.where(keep, 0.0, b)

    def add_placed(z, dst, blocks, dr, dc, y, x, weight):
        q = lax.div(x, H) + 4 * dc
        length = T if dr == 0 else M
        start = T - y - dr * T
        if dr != 0:
            start = jnp.minimum(start, 3 * M)
        for b in blocks:
            j = b - q
            inside = jnp.where((j >= 0) & (j <= 2), weight, 0.0).astype(F32)
            near = jnp.clip(j, 0, 2)
            for i in range(0, length, C):
                dst[b, i:i + C, :] += z[near, pl.ds(start + i, C), :] * inside

    def send_up(turn, ch):
        for s in range(2):
            y, x, _ = place_of(-1, 0, s)

            def store(i, b0, b1, s=s):
                out_up[s, ch, 0, i:i + C, :] = b0
                out_up[s, ch, 1, i:i + C, :] = b1

            extract(ch, jnp.maximum(y - T, -M) + M, x, store)
            pl.when(not_top)(lambda: up(turn, s, ch).start())

    first = [(ch, q) for half in range(2) for ch in range(2) for q in (2 * half, 2 * half + 1)]

    def first_piece(n):
        pl.when(not_left)(lambda: to_left(obj, 0, *first[n]).start())

    first_piece(0)
    first_piece(1)

    for load in later:
        load.wait()

    for s in range(2):
        value = meas[s]
        for step in range(2):
            h = value.astype(BF16)
            rest = value - h.astype(F32)
            m = rest.astype(BF16)
            low = (rest - m.astype(F32)).astype(BF16)
            if step == 0:
                value = (dot(pick[...], h) + dot(pick[...], m)) + dot(pick[...], low)
            else:
                value = (dot(h, pick_t[...]) + dot(m, pick_t[...])) + dot(low, pick_t[...])
        root[s] = jnp.sqrt(value)

    for n, (ch, q) in enumerate(first):
        with jax.named_scope("first_piece"):
            pl.when(not_right)(lambda: to_left(obj, 0, ch, q).wait_recv())
        if n + 2 < len(first):
            first_piece(n + 2)
        for b in range(2):
            for i in range(0, H, C):
                obj[ch, 4 + b, M + q * H + i:M + q * H + i + C, :] = hr[0, ch, q, b, i:i + C, :]
        if q == 1:
            send_up(0, ch)

    def take(it, s):
        y, x, live = place_of(0, 0, s)

        def store(i, b0, b1, ch):
            own = line + i < T - y
            parts = (b0, b1)
            for b in range(2):
                value = jnp.where(own, parts[b], vh[it, s, ch, b, i:i + C, :])
                patch[s, ch, i:i + C, b * H:(b + 1) * H] = value
                sum_ref(2, 0, b)[i:i + C, :] += value * value * live

        for ch in range(2):
            extract(ch, M + y, x, functools.partial(store, ch=ch))

    def slot(it, s):
        _, _, live = place_of(0, 0, s)
        cc, sc = twc[0], twc[1]
        lanes = (slice(0, H), slice(H, M))
        for k in range(2):
            for i in range(0, H, 16):
                cr, sr = twr[0, i:i + 16, :], twr[1, i:i + 16, :]
                for b in range(2):
                    er, ei = [], []
                    for t in (i, i + H):
                        at = (slice(t, t + 16), lanes[b])
                        pr, pi = patch[(s, 0) + at], patch[(s, 1) + at]
                        qr, qi = probe[(0, k) + at], probe[(1, k) + at]
                        er.append(qr * pr - qi * pi)
                        ei.append(qr * pi + qi * pr)
                        exits[(k, 0) + at] = er[-1]
                        exits[(k, 1) + at] = ei[-1]
                    dr, di = er[0] - er[1], ei[0] - ei[1]
                    store_parts(lop, k, i, b * H, 0, er[0] + er[1])
                    store_parts(lop, k, i + H, b * H, 0, ei[0] + ei[1])
                    store_parts(lop, k, i, M + b * H, 0, dr * cr + di * sr)
                    store_parts(lop, k, i + H, M + b * H, 0, di * cr - dr * sr)
            lout[k] = dot(wl[...], lop[k])
        for k in range(2):
            for i in range(0, M, 16):
                j, c = i % H, (i // H) * M
                lr = [lout[k, j:j + 16, c + b * H:c + b * H + H] for b in range(2)]
                li = [lout[k, j + H:j + H + 16, c + b * H:c + b * H + H] for b in range(2)]
                dr, di = lr[0] - lr[1], li[0] - li[1]
                store_parts(rop, k, i, 0, 1, lr[0] + lr[1])
                store_parts(rop, k, i, H, 1, li[0] + li[1])
                store_parts(rop, k, i + M, 0, 1, dr * cc + di * sc)
                store_parts(rop, k, i + M, H, 1, di * cc - dr * sc)
            rout[k] = dot(rop[k], wr[...])
        for i in range(0, 2 * M, 16):
            f = [[rout[k, i:i + 16, lanes[b]] for b in range(2)] for k in range(2)]
            model = (f[0][0] * f[0][0] + f[0][1] * f[0][1]) + (f[1][0] * f[1][0] + f[1][1] * f[1][1])
            scale = root[s, i % M:i % M + 16, lanes[i // M]]
            scale = scale * lax.rsqrt(jnp.maximum(model, MODEL_FLOOR))
            for k in range(2):
                for b in range(2):
                    store_parts(rop, k, i, b * H, 1, f[k][b] * scale)
        for k in range(2):
            rout[k] = dot(rop[k], wrb[...])
        for k in range(2):
            for i in range(0, M, 16):
                er, ei = rout[k, i:i + 16, lanes[0]], rout[k, i:i + 16, lanes[1]]
                dr, di = rout[k, i + M:i + M + 16, lanes[0]], rout[k, i + M:i + M + 16, lanes[1]]
                tr, ti = dr * cc - di * sc, di * cc + dr * sc
                j, c = i % H, (i // H) * M
                store_parts(lop, k, j, c, 0, er + tr)
                store_parts(lop, k, j, c + H, 0, er - tr)
                store_parts(lop, k, j + H, c, 0, ei + ti)
                store_parts(lop, k, j + H, c + H, 0, ei - ti)
            lout[k] = dot(wlb[...], lop[k])
        for i in range(0, H, 16):
            cr, sr = twr[0, i:i + 16, :], twr[1, i:i + 16, :]
            for b in range(2):
                u = [[None, None], [None, None]]
                for k in range(2):
                    c = b * H
                    er, ei = lout[k, i:i + 16, c:c + H], lout[k, i + H:i + H + 16, c:c + H]
                    dr = lout[k, i:i + 16, M + c:M + c + H]
                    di = lout[k, i + H:i + H + 16, M + c:M + c + H]
                    tr, ti = dr * cr - di * sr, di * cr + dr * sr
                    for n, (gr, gi) in enumerate(((er + tr, ei + ti), (er - tr, ei - ti))):
                        t = i + n * H
                        at = (slice(t, t + 16), lanes[b])
                        gr = (gr - exits[(k, 0) + at]) * live
                        gi = (gi - exits[(k, 1) + at]) * live
                        qr, qi = probe[(0, k) + at], probe[(1, k) + at]
                        pr, pi = patch[(s, 0) + at], patch[(s, 1) + at]
                        ur, ui = qr * gr + qi * gi, qr * gi - qi * gr
                        if k == 0:
                            u[n] = [ur, ui]
                        else:
                            upd[s, 0, b, t:t + 16, :] = u[n][0] + ur
                            upd[s, 1, b, t:t + 16, :] = u[n][1] + ui
                        sum_ref(k, 0, b)[t:t + 16, :] += pr * gr + pi * gi
                        sum_ref(k, 1, b)[t:t + 16, :] += pr * gi - pi * gr
        for ch in range(2):
            pl.when(not_bottom)(lambda: down(it, s, ch).start())

    def place(ch, dr, s, src):
        y, x, _ = place_of(dr, 0, s)
        spread(zbuf.at[ch], lambda i: (src[0, i:i + C, :], src[1, i:i + C, :]), x)
        add_placed(zbuf.at[ch], acc.at[ch], range(6), dr, 0, y, x, 1.0)

    def sum_ref(k, part, b):
        if k == 2:
            return ar[26].at[b]
        return ar[13 * k].at[part, pl.ds(b * M, M), :]

    def group(it, n, phase, axis, src, dst):
        ssem, rsem = ar[13 * n + 11], ar[13 * n + 12]
        out = []
        for d in range(1, size[axis]):
            j = lax.rem(me[axis] + d, size[axis])
            out.append(
                remote(src(j), dst, ssem.at[it, phase, d], rsem.at[it, phase, d], device(axis, j))
            )
        return out

    def phase_copies(it, n, phase):
        st = streams[n]
        own, cin, m0, r1, m1, r2, m2, r3, g2, g1, gc, ssem, rsem = ar[13 * n:13 * n + 13]
        a, b, c = st.axes
        R1, R2 = st.r1, st.r2
        rows_of = lambda j, r: pl.ds(pl.multiple_of(j * r, 8), r)
        if phase == 0:
            return [remote(own.at[1 - core], cin.at[it], ssem.at[it, 0, 0], rsem.at[it, 0, 0], partner)]
        if phase == 1:
            return group(it, n, 1, a, lambda j: m0.at[rows_of(j, R1), :], r1.at[it, me[a]])
        if phase == 2:
            return group(it, n, 2, b, lambda j: m1.at[rows_of(j, R2), :], r2.at[it, me[b]])
        if phase == 3:
            return group(it, n, 3, c, lambda j: m2, r3.at[it, me[c]])
        if phase == 4:
            part = g2.at[it, rows_of(me[b], R2), :]
            return group(it, n, 4, b, lambda j: part, part)
        if phase == 5:
            part = g1.at[it, rows_of(me[a], R1), :]
            return group(it, n, 5, a, lambda j: part, part)
        part = gc.at[it, core]
        return [remote(part, part, ssem.at[it, 6, 0], rsem.at[it, 6, 0], partner)]

    def ar_start(it, which):
        for n in which:
            for copy in phase_copies(it, n, 0):
                copy.start()

    def ar_step(it, which, phase):
        for n in which:
            st = streams[n]
            own, cin, m0, r1, m1, r2, m2, r3, g2, g1, gc, ssem, rsem = ar[13 * n:13 * n + 13]
            a, b, c = st.axes
            rows_of = lambda j, r: pl.ds(pl.multiple_of(j * r, 8), r)
            for copy in phase_copies(it, n, phase):
                copy.wait_recv()
            if phase == 0:
                for i in range(0, st.half, C):
                    m0[i:i + C, :] = own[core, i:i + C, :] + cin[it, i:i + C, :]
                r1[it, me[a]] = m0[rows_of(me[a], st.r1), :]
            elif phase == 1:
                m1[...] = functools.reduce(lambda p, q: p + q, [r1[it, j] for j in range(st.n[0])])
                r2[it, me[b]] = m1[rows_of(me[b], st.r2), :]
            elif phase == 2:
                m2[...] = functools.reduce(lambda p, q: p + q, [r2[it, j] for j in range(st.n[1])])
                r3[it, me[c]] = m2[...]
            elif phase == 3:
                g2[it, rows_of(me[b], st.r2), :] = functools.reduce(
                    lambda p, q: p + q, [r3[it, j] for j in range(st.n[2])]
                )
            elif phase == 4:
                g1[it, rows_of(me[a], st.r1), :] = g2[it]
            elif phase == 5:
                gc[it, core] = g1[it]
            if phase < 6:
                for copy in phase_copies(it, n, phase + 1):
                    copy.start()

    mode_sums, power_sum = (0, 1), (2,)

    def zero_sums():
        acc[...] = jnp.zeros_like(acc)
        for n in range(3):
            ar[13 * n][...] = jnp.zeros_like(ar[13 * n])

    def take_all(it):
        for s in range(2):
            take(it, s)
        ar_start(it, power_sum)

    def iteration(it, _):
        more = it < ITERS - 1
        send_left = not_left & more
        get_right = not_right & more
        scope = jax.named_scope

        def one(s, carry):
            slot(it, s)

            @pl.when(s == 0)
            def _():
                ar_step(it, power_sum, 0)

            return carry

        with scope("slots"):
            lax.fori_loop(0, 2, one, 0)
        ar_start(it, mode_sums)

        def send(ch, q):
            pl.when(not_right)(lambda: to_right(it, ch, q).start())
            pl.when(send_left)(lambda: to_left(acc, it + 1, ch, q).start())

        def arrive(ch, q):
            pl.when(not_left)(lambda: to_right(it, ch, q).wait_recv())
            pl.when(get_right)(lambda: to_left(acc, it + 1, ch, q).wait_recv())

        def update(ch, q):
            for i in range(q * H, q * H + H, C):
                rows, there, j = slice(i, i + C), slice(M + i, M + i + C), i - q * H
                for b in range(4):
                    step = acc[ch, b, rows, :]
                    if b < 2:
                        step = step + hl[it, ch, q, b, j:j + C, :]
                    obj[ch, b, there, :] += step * den[b, rows, :]

            @pl.when(get_right)
            def _():
                for i in range(q * H, q * H + H, C):
                    rows, there, j = slice(i, i + C), slice(M + i, M + i + C), i - q * H
                    for b in range(2):
                        step = acc[ch, 4 + b, rows, :] + hr[it + 1, ch, q, b, j:j + C, :]
                        obj[ch, 4 + b, there, :] += step * den[4 + b, rows, :]

        def clear(it):
            for ch in range(2):
                for q in range(4):
                    pl.when(not_right)(lambda: to_right(it, ch, q).wait_send())
                    pl.when(send_left)(lambda: to_left(acc, it + 1, ch, q).wait_send())
            for n in range(len(streams)):
                for copy in phase_copies(it, n, 0):
                    copy.wait_send()
            zero_sums()

        def below(s, ch):
            pl.when(not_top)(lambda: down(it, s, ch).wait_recv())
            place(ch, -1, s, vu.at[it, s, ch])

        for ch in range(2):
            for s in range(2):
                place(ch, 0, s, upd.at[s, ch])
            if ch == 0:
                send(0, 2)
                send(0, 3)
        with scope("core_sums"):
            ar_step(it, power_sum, 1)
            ar_step(it, mode_sums, 0)
        with scope("from_above"):
            for q in range(2):
                if q == 0:
                    below(0, 0)
                    below(1, 0)
                arrive(0, 2 + q)
                send(0, q)
            below(0, 1)
            below(1, 1)
        ar_step(it, power_sum, 2)

        with scope("coverage"):
            power_all = jnp.zeros((C, H), F32)
            for b in range(2):
                for i in range(0, M, C):
                    at = (slice(i, i + C), slice(b * H, b * H + H))
                    square = (
                        probe[(0, 0) + at] ** 2 + probe[(1, 0) + at] ** 2
                        + probe[(0, 1) + at] ** 2 + probe[(1, 1) + at] ** 2
                    )
                    power[b, i:i + C, :] = square
                    power_all = power_all + square
            reg_object = DAMPING * (jnp.sum(power_all) * (1.0 / (M * M))) + SMALL
            den[...] = jnp.zeros_like(den)
            for dr in (0, -1):
                for dc, blocks in ((0, range(6)), (-1, range(2)), (1, range(4, 6))):

                    def cover(s, carry, dr=dr, dc=dc, blocks=blocks):
                        y, x, live = place_of(dr, dc, s)
                        spread(cbuf, lambda i: (power[0, i:i + C, :], power[1, i:i + C, :]), x)
                        add_placed(cbuf, den, blocks, dr, dc, y, x, live)
                        return carry

                    lax.fori_loop(0, 2, cover, 0)
            for b in range(6):
                for i in range(0, T, C):
                    den[b, i:i + C, :] = 1.0 / (den[b, i:i + C, :] + reg_object)

        with scope("piece_00"):
            arrive(0, 0)
        send(1, 0)
        update(0, 0)
        with scope("first_split"):
            ar_step(it, mode_sums, 1)
        with scope("piece_01"):
            arrive(0, 1)
        send(1, 1)
        update(0, 1)
        pl.when(more)(lambda: send_up(it + 1, 0))
        ar_step(it, power_sum, 3)
        with scope("second_split"):
            ar_step(it, mode_sums, 2)
        with scope("piece_10"):
            arrive(1, 0)
        send(1, 2)
        update(1, 0)
        with scope("exchange"):
            ar_step(it, mode_sums, 3)
        with scope("piece_11"):
            arrive(1, 1)
        send(1, 3)
        update(1, 1)
        pl.when(more)(lambda: send_up(it + 1, 1))
        update(0, 2)
        update(0, 3)
        ar_step(it, power_sum, 4)
        with scope("first_gather"):
            ar_step(it, mode_sums, 4)
        with scope("piece_12"):
            arrive(1, 2)
        update(1, 2)
        ar_step(it, power_sum, 5)
        with scope("piece_13"):
            arrive(1, 3)
        update(1, 3)
        clear(it)

        @pl.when(more)
        def _():
            with scope("from_below"):
                for ch in range(2):
                    for s in range(2):
                        pl.when(not_bottom)(lambda: up(it + 1, s, ch).wait_recv())
            take_all(it + 1)

        with scope("second_gather"):
            ar_step(it, mode_sums, 5)
        with scope("core_gather"):
            for n in range(len(streams)):
                for copy in phase_copies(it, n, 6):
                    copy.wait_recv()

        def total(k, part, b, i):
            if k == 2:
                return ar[36][it, b, i:i + C, :]
            return ar[13 * k + 10][it, part, b * M + i:b * M + i + C, :]

        sums = jnp.zeros((C, H), F32)
        for b in range(2):
            for i in range(0, M, C):
                sums = sums + total(2, 0, b, i)
        reg_probe = DAMPING * (jnp.sum(sums) * (1.0 / (M * M))) + SMALL
        for b in range(2):
            for i in range(0, M, C):
                scale = 1.0 / (total(2, 0, b, i) + reg_probe)
                for k in range(2):
                    for part in range(2):
                        at = (part, k, slice(i, i + C), slice(b * H, b * H + H))
                        probe[at] += total(k, part, b, i) * scale

        for n in range(len(streams)):
            for phase in range(1, 7):
                for copy in phase_copies(it, n, phase):
                    copy.wait_send()
        for ch in range(2):
            for s in range(2):
                pl.when(not_bottom)(lambda: down(it, s, ch).wait_send())
                pl.when(not_top & more)(lambda: up(it + 1, s, ch).wait_send())
        return 0

    for ch in range(2):
        for q in range(4):
            pl.when(not_left)(lambda: to_left(obj, 0, ch, q).wait_send())
        for s in range(2):
            pl.when(not_bottom)(lambda: up(0, s, ch).wait_recv())
            pl.when(not_top)(lambda: up(0, s, ch).wait_send())

    zero_sums()
    take_all(0)
    lax.fori_loop(0, ITERS, iteration, 0)

    stores = []
    for ch in range(2):
        for b in range(4):
            store = pltpu.make_async_copy(
                obj.at[ch, b, pl.ds(M, T), :], obj_out.at[ch, :, pl.ds(b * H, H)], io_sem.at[ch, b]
            )
            store.start()
            stores.append(store)
    for store in stores:
        store.wait()


def shards(rows_n, cols_n, nz, ny, object_field, probe_modes, intensities, positions, counts):
    sizes = {"x": rows_n // 2, "y": ny, "z": nz}
    streams = (
        Stream(1024, ("x", "z", "y"), sizes),
        Stream(1024, ("x", "y", "z"), sizes),
        Stream(512, ("x", "z", "y"), sizes),
    )
    vm = lambda *shape: pltpu.VMEM(shape, F32)
    sem = lambda *shape: pltpu.SemaphoreType.DMA(shape)
    consts = [jnp.asarray(t) for t in tables()]
    scratch = [vm(2, M, M)] + [pltpu.VMEM(t.shape, t.dtype) for t in consts]
    scratch += [
        vm(2, 6, 1024, H),
        vm(2, 6, T, H),
        vm(6, T, H),
        vm(2, 3, 1024, H),
        vm(3, 1024, H),
        vm(2, M, H),
        vm(2, 2, M, M),
        vm(2, 2, M, M),
        pltpu.VMEM((2, 3 * M, 2 * M), BF16),
        vm(2, M, 2 * M),
        pltpu.VMEM((2, 2 * M, 3 * M), BF16),
        vm(2, 2 * M, M),
        vm(2, M, M),
        vm(2, 2, 2, M, H),
        vm(2, 2, 2, M, H),
        vm(ITERS, 2, 4, 2, H, H),
        vm(ITERS, 2, 4, 2, H, H),
        vm(ITERS, 2, 2, 2, M, H),
        vm(ITERS, 2, 2, 2, M, H),
        sem(10),
        sem(2, 4),
        sem(ITERS, 2, 2, 4),
        sem(ITERS, 2, 2, 4),
        sem(ITERS, 2, 2),
        sem(ITERS, 2, 2),
        sem(ITERS, 2, 2),
        sem(ITERS, 2, 2),
    ]
    for st in streams:
        scratch += st.scratch()
    smem = pl.BlockSpec(memory_space=pltpu.SMEM)
    vmem = pl.BlockSpec(memory_space=pltpu.VMEM)
    hbm = pl.BlockSpec(memory_space=pl.ANY)
    return pl.pallas_call(
        functools.partial(kernel, rows_n, cols_n, nz, ny, streams),
        out_shape=(
            jax.ShapeDtypeStruct((2, T, T), F32),
            jax.ShapeDtypeStruct((2, 2, M, M), F32),
        ),
        in_specs=[smem, smem, hbm, hbm, hbm] + [hbm] * len(consts),
        out_specs=(hbm, vmem),
        scratch_shapes=scratch,
        compiler_params=pltpu.CompilerParams(
            collective_id=0, has_side_effects=True, vmem_limit_bytes=62 * 1024 * 1024
        ),
        name="ptycho",
    )(positions.T, counts, object_field, probe_modes, intensities, *consts)


def solution(mesh):
    rows_n, cols_n = mesh.shape["row"], mesh.shape["col"]
    ny = math.isqrt(cols_n)
    nz = cols_n // ny
    placed = (P(None, "row", "col"), P(), P(("row", "col"), None, None), P(), P())
    return jax.shard_map(
        functools.partial(shards, rows_n, cols_n, nz, ny),
        mesh=mesh,
        in_specs=placed,
        out_specs=(P(None, "row", "col"), P()),
        check_vma=False,
    )
```

```python
import functools
import math

import jax
import jax.numpy as jnp
import ml_dtypes
import numpy as np
from jax import lax
from jax.experimental import pallas as pl
from jax.experimental.pallas import tpu as pltpu
from jax.sharding import PartitionSpec as P

ITERS = 3
M = 256
H = 128
T = 512
MODEL_FLOOR = 0.5
DAMPING = 0.2
SMALL = 1e-06
MESH = pl.DeviceIdType.MESH
F32 = jnp.float32
BF16 = jnp.bfloat16


def tables():
    k = np.arange(H)
    angle = 2.0 * np.pi * ((k[:, None] * k[None, :]) % H) / H
    c, s = np.cos(angle) / 16.0, np.sin(angle) / 16.0

    def three(matrix, axis):
        wide = matrix.astype(np.float32)
        hi = wide.astype(ml_dtypes.bfloat16)
        lo = (wide - hi.astype(np.float32)).astype(ml_dtypes.bfloat16)
        return np.concatenate([hi, hi, lo], axis=axis)

    left = np.block([[c, s], [-s, c]])
    left_back = np.block([[c, -s], [s, c]])
    turn = 2.0 * np.pi * k / M
    rows = np.stack([np.cos(turn), np.sin(turn)])[:, :, None] * np.ones((1, 1, H))
    cols = rows.transpose(0, 2, 1)[:, :16]
    order = np.concatenate([np.arange(0, M, 2), np.arange(1, M, 2)])
    pick = np.zeros((M, M), np.float32)
    pick[np.arange(M), order] = 1.0
    return (
        three(left, 1),
        three(left_back, 1),
        three(left.T, 0),
        three(left_back.T, 0),
        rows.astype(np.float32),
        cols.astype(np.float32),
        pick.astype(ml_dtypes.bfloat16),
        np.ascontiguousarray(pick.T).astype(ml_dtypes.bfloat16),
    )


def dot(a, b):
    return jnp.dot(a, b, preferred_element_type=F32)


def cat(parts, axis):
    return jnp.concatenate(parts, axis=axis)


def split(x):
    hi = x.astype(BF16)
    lo = (x - hi.astype(F32)).astype(BF16)
    return hi, lo


def store_parts(ref, k, row, lane, axis, x):
    hi, lo = split(x)
    for n, part in enumerate((hi, lo, hi)):
        r, c = (row + n * M, lane) if axis == 0 else (row, lane + n * M)
        ref[k, r:r + 16, c:c + H] = part


class Stream:
    def __init__(self, rows, axes, sizes):
        self.half = rows // 2
        self.axes = axes
        self.n = [sizes[a] for a in axes]
        self.r1 = self.half // self.n[0]
        self.r2 = self.r1 // self.n[1]

    def scratch(self):
        vm = lambda *shape: pltpu.VMEM(shape, F32)
        n1, n2, n3 = self.n
        return [
            vm(2, self.half, H),
            vm(ITERS, self.half, H),
            vm(self.half, H),
            vm(ITERS, n1, self.r1, H),
            vm(self.r1, H),
            vm(ITERS, n2, self.r2, H),
            vm(self.r2, H),
            vm(ITERS, n3, self.r2, H),
            vm(ITERS, self.r1, H),
            vm(ITERS, self.half, H),
            vm(ITERS, 2, self.half, H),
            pltpu.SemaphoreType.DMA((ITERS, 7, 4)),
            pltpu.SemaphoreType.DMA((ITERS, 7, 4)),
        ]


def kernel(
    rows_n, cols_n, nz, ny, streams,
    pos, counts, obj_in, probe_in, meas_in, wl_in, wlb_in, wr_in, wrb_in, twr_in, twc_in, pick_in,
    pick_t_in, obj_out, probe,
    meas, wl, wlb, wr, wrb, twr, twc, pick, pick_t,
    obj, acc, den, zbuf, cbuf, power, patch, exits, lop, lout, rop, rout, root, upd, out_up,
    hr, hl, vu, vh,
    load_sem, io_sem, hs, hrs, vs, vrs, us, urs, *ar,
):
    nx = rows_n // 2
    row, col = lax.axis_index("row"), lax.axis_index("col")
    core, xi = lax.rem(row, 2), lax.div(row, 2)
    yi, zi = lax.rem(col, ny), lax.div(col, ny)
    me = {"x": xi, "y": yi, "z": zi}
    size = {"x": nx, "y": ny, "z": nz}

    def device(axis, j):
        if axis == "x":
            return (j * 2 + core, col)
        if axis == "y":
            return (row, zi * ny + j)
        return (row, j * ny + yi)

    partner = (row + 1 - 2 * core, col)
    not_left, not_right = col > 0, col < cols_n - 1
    not_top, not_bottom = row > 0, row < rows_n - 1

    loads = []
    for ch in range(2):
        for b in range(4):
            load = pltpu.make_async_copy(
                obj_in.at[ch, :, pl.ds(b * H, H)], obj.at[ch, b, pl.ds(M, T), :], io_sem.at[ch, b]
            )
            load.start()
            loads.append(load)
    later = []
    for i, (src, dst) in enumerate(
        (
            (meas_in, meas), (pick_in, pick), (pick_t_in, pick_t), (probe_in, probe), (wl_in, wl),
            (wlb_in, wlb), (wr_in, wr), (wrb_in, wrb), (twr_in, twr), (twc_in, twc),
        )
    ):
        load = pltpu.make_async_copy(src, dst, load_sem.at[i])
        load.start()
        later.append(load)

    barrier = pltpu.get_barrier_semaphore()

    def greet(who):
        pl.semaphore_signal(barrier, inc=1, device_id=who, device_id_type=MESH)

    greet(partner)
    peers = 1
    for axis in ("z", "y", "x"):
        for d in range(1, size[axis]):
            greet(device(axis, lax.rem(me[axis] + d, size[axis])))
            peers += 1
    pl.when(not_left)(lambda: greet((row, col - 1)))
    pl.when(not_right)(lambda: greet((row, col + 1)))
    pl.when(not_top)(lambda: greet((row - 1, col)))
    pl.when(not_bottom)(lambda: greet((row + 1, col)))

    zbuf[...] = jnp.zeros_like(zbuf)
    cbuf[...] = jnp.zeros_like(cbuf)

    @pl.when(jnp.logical_not(not_left))
    def _():
        hl[...] = jnp.zeros_like(hl)

    @pl.when(jnp.logical_not(not_right))
    def _():
        hr[...] = jnp.zeros_like(hr)

    @pl.when(jnp.logical_not(not_top))
    def _():
        vu[...] = jnp.zeros_like(vu)

    @pl.when(jnp.logical_not(not_bottom))
    def _():
        vh[...] = jnp.zeros_like(vh)

    for load in loads:
        load.wait()
    pl.semaphore_wait(
        barrier,
        peers
        + not_left.astype(jnp.int32) + not_right.astype(jnp.int32)
        + not_top.astype(jnp.int32) + not_bottom.astype(jnp.int32),
    )

    def remote(src, dst, send, recv, who):
        return pltpu.make_async_remote_copy(
            src_ref=src, dst_ref=dst, send_sem=send, recv_sem=recv, device_id=who, device_id_type=MESH
        )

    def to_left(src, turn, ch, q):
        base = M if src is obj else 0
        return remote(
            src.at[ch, pl.ds(0, 2), pl.ds(base + q * H, H), :], hr.at[turn, ch, q],
            hs.at[turn, 0, ch, q], hrs.at[turn, 0, ch, q], (row, col - 1),
        )

    def to_right(turn, ch, q):
        return remote(
            acc.at[ch, pl.ds(4, 2), pl.ds(q * H, H), :], hl.at[turn, ch, q],
            hs.at[turn, 1, ch, q], hrs.at[turn, 1, ch, q], (row, col + 1),
        )

    def down(it, s, ch):
        return remote(
            upd.at[s, ch], vu.at[it, s, ch], us.at[it, s, ch], urs.at[it, s, ch], (row + 1, col)
        )

    def up(turn, s, ch):
        return remote(
            out_up.at[s, ch], vh.at[turn, s, ch], vs.at[turn, s, ch], vrs.at[turn, s, ch],
            (row - 1, col),
        )

    C = 64
    lane = lax.broadcasted_iota(jnp.int32, (C, H), 1)
    line = lax.broadcasted_iota(jnp.int32, (C, H), 0)

    def place_of(dr, dc, s):
        r, c = row + dr, col + dc
        there = (r >= 0) & (r < rows_n) & (c >= 0) & (c < cols_n)
        r, c = jnp.clip(r, 0, rows_n - 1), jnp.clip(c, 0, cols_n - 1)
        dev = r * cols_n + c
        y = jnp.clip(pos[0, dev * 2 + s] - r * T, 0, T - 1)
        x = jnp.clip(pos[1, dev * 2 + s] - c * T, 0, T - 1)
        live = jnp.where(there & (s < counts[dev]), 1.0, 0.0).astype(F32)
        return y, x, live

    def extract(ch, start, x, store):
        q, r = lax.div(x, H), lax.rem(x, H)
        back = lax.rem(H - r, H)
        keep = lane < H - r
        for i in range(0, M, C):
            b = [pltpu.roll(obj[ch, q + j, pl.ds(start + i, C), :], back, 1) for j in range(3)]
            store(i, jnp.where(keep, b[0], b[1]), jnp.where(keep, b[1], b[2]))

    def spread(z, load, x):
        r = lax.rem(x, H)
        keep = lane >= r
        for i in range(0, M, C):
            u0, u1 = load(i)
            a, b = pltpu.roll(u0, r, 1), pltpu.roll(u1, r, 1)
            z[0, T + i:T + i + C, :] = jnp.where(keep, a, 0.0)
            z[1, T + i:T + i + C, :] = jnp.where(keep, b, a)
            z[2, T + i:T + i + C, :] = jnp.where(keep, 0.0, b)

    def add_placed(z, dst, blocks, dr, dc, y, x, weight):
        q = lax.div(x, H) + 4 * dc
        length = T if dr == 0 else M
        start = T - y - dr * T
        if dr != 0:
            start = jnp.minimum(start, 3 * M)
        for b in blocks:
            j = b - q
            inside = jnp.where((j >= 0) & (j <= 2), weight, 0.0).astype(F32)
            near = jnp.clip(j, 0, 2)
            for i in range(0, length, C):
                dst[b, i:i + C, :] += z[near, pl.ds(start + i, C), :] * inside

    def send_up(turn, ch):
        for s in range(2):
            y, x, _ = place_of(-1, 0, s)

            def store(i, b0, b1, s=s):
                out_up[s, ch, 0, i:i + C, :] = b0
                out_up[s, ch, 1, i:i + C, :] = b1

            extract(ch, jnp.maximum(y - T, -M) + M, x, store)
            pl.when(not_top)(lambda: up(turn, s, ch).start())

    first = [(ch, q) for half in range(2) for ch in range(2) for q in (2 * half, 2 * half + 1)]

    def first_piece(n):
        pl.when(not_left)(lambda: to_left(obj, 0, *first[n]).start())

    first_piece(0)
    first_piece(1)

    for load in later:
        load.wait()

    for s in range(2):
        value = meas[s]
        for step in range(2):
            h = value.astype(BF16)
            rest = value - h.astype(F32)
            m = rest.astype(BF16)
            low = (rest - m.astype(F32)).astype(BF16)
            if step == 0:
                value = (dot(pick[...], h) + dot(pick[...], m)) + dot(pick[...], low)
            else:
                value = (dot(h, pick_t[...]) + dot(m, pick_t[...])) + dot(low, pick_t[...])
        root[s] = jnp.sqrt(value)

    for n, (ch, q) in enumerate(first):
        with jax.named_scope("first_piece"):
            pl.when(not_right)(lambda: to_left(obj, 0, ch, q).wait_recv())
        if n + 2 < len(first):
            first_piece(n + 2)
        for b in range(2):
            for i in range(0, H, C):
                obj[ch, 4 + b, M + q * H + i:M + q * H + i + C, :] = hr[0, ch, q, b, i:i + C, :]
        if q == 1:
            send_up(0, ch)

    def take(it, s):
        y, x, live = place_of(0, 0, s)

        def store(i, b0, b1, ch):
            own = line + i < T - y
            parts = (b0, b1)
            for b in range(2):
                value = jnp.where(own, parts[b], vh[it, s, ch, b, i:i + C, :])
                patch[s, ch, i:i + C, b * H:(b + 1) * H] = value
                sum_ref(2, 0, b)[i:i + C, :] += value * value * live

        for ch in range(2):
            extract(ch, M + y, x, functools.partial(store, ch=ch))

    def slot(it, s):
        _, _, live = place_of(0, 0, s)
        cc, sc = twc[0], twc[1]
        lanes = (slice(0, H), slice(H, M))
        for k in range(2):
            for i in range(0, H, 16):
                cr, sr = twr[0, i:i + 16, :], twr[1, i:i + 16, :]
                for b in range(2):
                    er, ei = [], []
                    for t in (i, i + H):
                        at = (slice(t, t + 16), lanes[b])
                        pr, pi = patch[(s, 0) + at], patch[(s, 1) + at]
                        qr, qi = probe[(0, k) + at], probe[(1, k) + at]
                        er.append(qr * pr - qi * pi)
                        ei.append(qr * pi + qi * pr)
                        exits[(k, 0) + at] = er[-1]
                        exits[(k, 1) + at] = ei[-1]
                    dr, di = er[0] - er[1], ei[0] - ei[1]
                    store_parts(lop, k, i, b * H, 0, er[0] + er[1])
                    store_parts(lop, k, i + H, b * H, 0, ei[0] + ei[1])
                    store_parts(lop, k, i, M + b * H, 0, dr * cr + di * sr)
                    store_parts(lop, k, i + H, M + b * H, 0, di * cr - dr * sr)
            lout[k] = dot(wl[...], lop[k])
        for k in range(2):
            for i in range(0, M, 16):
                j, c = i % H, (i // H) * M
                lr = [lout[k, j:j + 16, c + b * H:c + b * H + H] for b in range(2)]
                li = [lout[k, j + H:j + H + 16, c + b * H:c + b * H + H] for b in range(2)]
                dr, di = lr[0] - lr[1], li[0] - li[1]
                store_parts(rop, k, i, 0, 1, lr[0] + lr[1])
                store_parts(rop, k, i, H, 1, li[0] + li[1])
                store_parts(rop, k, i + M, 0, 1, dr * cc + di * sc)
                store_parts(rop, k, i + M, H, 1, di * cc - dr * sc)
            rout[k] = dot(rop[k], wr[...])
        for i in range(0, 2 * M, 16):
            f = [[rout[k, i:i + 16, lanes[b]] for b in range(2)] for k in range(2)]
            model = (f[0][0] * f[0][0] + f[0][1] * f[0][1]) + (f[1][0] * f[1][0] + f[1][1] * f[1][1])
            scale = root[s, i % M:i % M + 16, lanes[i // M]]
            scale = scale * lax.rsqrt(jnp.maximum(model, MODEL_FLOOR))
            for k in range(2):
                for b in range(2):
                    store_parts(rop, k, i, b * H, 1, f[k][b] * scale)
        for k in range(2):
            rout[k] = dot(rop[k], wrb[...])
        for k in range(2):
            for i in range(0, M, 16):
                er, ei = rout[k, i:i + 16, lanes[0]], rout[k, i:i + 16, lanes[1]]
                dr, di = rout[k, i + M:i + M + 16, lanes[0]], rout[k, i + M:i + M + 16, lanes[1]]
                tr, ti = dr * cc - di * sc, di * cc + dr * sc
                j, c = i % H, (i // H) * M
                store_parts(lop, k, j, c, 0, er + tr)
                store_parts(lop, k, j, c + H, 0, er - tr)
                store_parts(lop, k, j + H, c, 0, ei + ti)
                store_parts(lop, k, j + H, c + H, 0, ei - ti)
            lout[k] = dot(wlb[...], lop[k])
        for i in range(0, H, 16):
            cr, sr = twr[0, i:i + 16, :], twr[1, i:i + 16, :]
            for b in range(2):
                u = [[None, None], [None, None]]
                for k in range(2):
                    c = b * H
                    er, ei = lout[k, i:i + 16, c:c + H], lout[k, i + H:i + H + 16, c:c + H]
                    dr = lout[k, i:i + 16, M + c:M + c + H]
                    di = lout[k, i + H:i + H + 16, M + c:M + c + H]
                    tr, ti = dr * cr - di * sr, di * cr + dr * sr
                    for n, (gr, gi) in enumerate(((er + tr, ei + ti), (er - tr, ei - ti))):
                        t = i + n * H
                        at = (slice(t, t + 16), lanes[b])
                        gr = (gr - exits[(k, 0) + at]) * live
                        gi = (gi - exits[(k, 1) + at]) * live
                        qr, qi = probe[(0, k) + at], probe[(1, k) + at]
                        pr, pi = patch[(s, 0) + at], patch[(s, 1) + at]
                        ur, ui = qr * gr + qi * gi, qr * gi - qi * gr
                        if k == 0:
                            u[n] = [ur, ui]
                        else:
                            upd[s, 0, b, t:t + 16, :] = u[n][0] + ur
                            upd[s, 1, b, t:t + 16, :] = u[n][1] + ui
                        sum_ref(k, 0, b)[t:t + 16, :] += pr * gr + pi * gi
                        sum_ref(k, 1, b)[t:t + 16, :] += pr * gi - pi * gr
        for ch in range(2):
            pl.when(not_bottom)(lambda: down(it, s, ch).start())

    def place(ch, dr, s, src):
        y, x, _ = place_of(dr, 0, s)
        spread(zbuf.at[ch], lambda i: (src[0, i:i + C, :], src[1, i:i + C, :]), x)
        add_placed(zbuf.at[ch], acc.at[ch], range(6), dr, 0, y, x, 1.0)

    def sum_ref(k, part, b):
        if k == 2:
            return ar[26].at[b]
        return ar[13 * k].at[part, pl.ds(b * M, M), :]

    def group(it, n, phase, axis, src, dst):
        ssem, rsem = ar[13 * n + 11], ar[13 * n + 12]
        out = []
        for d in range(1, size[axis]):
            j = lax.rem(me[axis] + d, size[axis])
            out.append(
                remote(src(j), dst, ssem.at[it, phase, d], rsem.at[it, phase, d], device(axis, j))
            )
        return out

    def phase_copies(it, n, phase):
        st = streams[n]
        own, cin, m0, r1, m1, r2, m2, r3, g2, g1, gc, ssem, rsem = ar[13 * n:13 * n + 13]
        a, b, c = st.axes
        R1, R2 = st.r1, st.r2
        rows_of = lambda j, r: pl.ds(pl.multiple_of(j * r, 8), r)
        if phase == 0:
            return [remote(own.at[1 - core], cin.at[it], ssem.at[it, 0, 0], rsem.at[it, 0, 0], partner)]
        if phase == 1:
            return group(it, n, 1, a, lambda j: m0.at[rows_of(j, R1), :], r1.at[it, me[a]])
        if phase == 2:
            return group(it, n, 2, b, lambda j: m1.at[rows_of(j, R2), :], r2.at[it, me[b]])
        if phase == 3:
            return group(it, n, 3, c, lambda j: m2, r3.at[it, me[c]])
        if phase == 4:
            part = g2.at[it, rows_of(me[b], R2), :]
            return group(it, n, 4, b, lambda j: part, part)
        if phase == 5:
            part = g1.at[it, rows_of(me[a], R1), :]
            return group(it, n, 5, a, lambda j: part, part)
        part = gc.at[it, core]
        return [remote(part, part, ssem.at[it, 6, 0], rsem.at[it, 6, 0], partner)]

    def ar_start(it, which):
        for n in which:
            for copy in phase_copies(it, n, 0):
                copy.start()

    def ar_step(it, which, phase):
        for n in which:
            st = streams[n]
            own, cin, m0, r1, m1, r2, m2, r3, g2, g1, gc, ssem, rsem = ar[13 * n:13 * n + 13]
            a, b, c = st.axes
            rows_of = lambda j, r: pl.ds(pl.multiple_of(j * r, 8), r)
            for copy in phase_copies(it, n, phase):
                copy.wait_recv()
            if phase == 0:
                for i in range(0, st.half, C):
                    m0[i:i + C, :] = own[core, i:i + C, :] + cin[it, i:i + C, :]
                r1[it, me[a]] = m0[rows_of(me[a], st.r1), :]
            elif phase == 1:
                m1[...] = functools.reduce(lambda p, q: p + q, [r1[it, j] for j in range(st.n[0])])
                r2[it, me[b]] = m1[rows_of(me[b], st.r2), :]
            elif phase == 2:
                m2[...] = functools.reduce(lambda p, q: p + q, [r2[it, j] for j in range(st.n[1])])
                r3[it, me[c]] = m2[...]
            elif phase == 3:
                g2[it, rows_of(me[b], st.r2), :] = functools.reduce(
                    lambda p, q: p + q, [r3[it, j] for j in range(st.n[2])]
                )
            elif phase == 4:
                g1[it, rows_of(me[a], st.r1), :] = g2[it]
            elif phase == 5:
                gc[it, core] = g1[it]
            if phase < 6:
                for copy in phase_copies(it, n, phase + 1):
                    copy.start()

    mode_sums, power_sum = (0, 1), (2,)

    def zero_sums():
        acc[...] = jnp.zeros_like(acc)
        for n in range(3):
            ar[13 * n][...] = jnp.zeros_like(ar[13 * n])

    def take_all(it):
        for s in range(2):
            take(it, s)
        ar_start(it, power_sum)

    def iteration(it, _):
        more = it < ITERS - 1
        send_left = not_left & more
        get_right = not_right & more
        scope = jax.named_scope

        def one(s, carry):
            slot(it, s)

            @pl.when(s == 0)
            def _():
                ar_step(it, power_sum, 0)

            return carry

        with scope("slots"):
            lax.fori_loop(0, 2, one, 0)
        ar_start(it, mode_sums)

        def send(ch, q):
            pl.when(not_right & (core == 0))(lambda: to_right(it, ch, q).start())
            pl.when(send_left)(lambda: to_left(acc, it + 1, ch, q).start())
            pl.when(not_right & (core == 1))(lambda: to_right(it, ch, q).start())

        def arrive(ch, q):
            pl.when(not_left)(lambda: to_right(it, ch, q).wait_recv())
            pl.when(get_right)(lambda: to_left(acc, it + 1, ch, q).wait_recv())

        def update(ch, q):
            for i in range(q * H, q * H + H, C):
                rows, there, j = slice(i, i + C), slice(M + i, M + i + C), i - q * H
                for b in range(4):
                    step = acc[ch, b, rows, :]
                    if b < 2:
                        step = step + hl[it, ch, q, b, j:j + C, :]
                    obj[ch, b, there, :] += step * den[b, rows, :]

            @pl.when(get_right)
            def _():
                for i in range(q * H, q * H + H, C):
                    rows, there, j = slice(i, i + C), slice(M + i, M + i + C), i - q * H
                    for b in range(2):
                        step = acc[ch, 4 + b, rows, :] + hr[it + 1, ch, q, b, j:j + C, :]
                        obj[ch, 4 + b, there, :] += step * den[4 + b, rows, :]

        def clear(it):
            for ch in range(2):
                for q in range(4):
                    pl.when(not_right)(lambda: to_right(it, ch, q).wait_send())
                    pl.when(send_left)(lambda: to_left(acc, it + 1, ch, q).wait_send())
            for n in range(len(streams)):
                for copy in phase_copies(it, n, 0):
                    copy.wait_send()
            zero_sums()

        def below(s, ch):
            pl.when(not_top)(lambda: down(it, s, ch).wait_recv())
            place(ch, -1, s, vu.at[it, s, ch])

        for ch in range(2):
            for s in range(2):
                place(ch, 0, s, upd.at[s, ch])
            if ch == 0:
                send(0, 2)
                send(0, 3)
        with scope("core_sums"):
            ar_step(it, power_sum, 1)
            ar_step(it, mode_sums, 0)
        with scope("from_above"):
            for q in range(2):
                if q == 0:
                    below(0, 0)
                    below(1, 0)
                arrive(0, 2 + q)
                send(0, q)
            below(0, 1)
            below(1, 1)
        ar_step(it, power_sum, 2)

        with scope("coverage"):
            power_all = jnp.zeros((C, H), F32)
            for b in range(2):
                for i in range(0, M, C):
                    at = (slice(i, i + C), slice(b * H, b * H + H))
                    square = (
                        probe[(0, 0) + at] ** 2 + probe[(1, 0) + at] ** 2
                        + probe[(0, 1) + at] ** 2 + probe[(1, 1) + at] ** 2
                    )
                    power[b, i:i + C, :] = square
                    power_all = power_all + square
            reg_object = DAMPING * (jnp.sum(power_all) * (1.0 / (M * M))) + SMALL
            den[...] = jnp.zeros_like(den)
            for dr in (0, -1):
                for dc, blocks in ((0, range(6)), (-1, range(2)), (1, range(4, 6))):

                    def cover(s, carry, dr=dr, dc=dc, blocks=blocks):
                        y, x, live = place_of(dr, dc, s)
                        spread(cbuf, lambda i: (power[0, i:i + C, :], power[1, i:i + C, :]), x)
                        add_placed(cbuf, den, blocks, dr, dc, y, x, live)
                        return carry

                    lax.fori_loop(0, 2, cover, 0)
            for b in range(6):
                for i in range(0, T, C):
                    den[b, i:i + C, :] = 1.0 / (den[b, i:i + C, :] + reg_object)

        with scope("piece_00"):
            arrive(0, 0)
        send(1, 0)
        update(0, 0)
        with scope("first_split"):
            ar_step(it, mode_sums, 1)
        with scope("piece_01"):
            arrive(0, 1)
        send(1, 1)
        update(0, 1)
        pl.when(more)(lambda: send_up(it + 1, 0))
        ar_step(it, power_sum, 3)
        with scope("second_split"):
            ar_step(it, mode_sums, 2)
        with scope("piece_10"):
            arrive(1, 0)
        send(1, 2)
        update(1, 0)
        with scope("exchange"):
            ar_step(it, mode_sums, 3)
        with scope("piece_11"):
            arrive(1, 1)
        send(1, 3)
        update(1, 1)
        pl.when(more)(lambda: send_up(it + 1, 1))
        update(0, 2)
        update(0, 3)
        ar_step(it, power_sum, 4)
        with scope("first_gather"):
            ar_step(it, mode_sums, 4)
        with scope("piece_12"):
            arrive(1, 2)
        update(1, 2)
        ar_step(it, power_sum, 5)
        with scope("piece_13"):
            arrive(1, 3)
        update(1, 3)
        clear(it)

        @pl.when(more)
        def _():
            with scope("from_below"):
                for ch in range(2):
                    for s in range(2):
                        pl.when(not_bottom)(lambda: up(it + 1, s, ch).wait_recv())
            take_all(it + 1)

        with scope("second_gather"):
            ar_step(it, mode_sums, 5)
        with scope("core_gather"):
            for n in range(len(streams)):
                for copy in phase_copies(it, n, 6):
                    copy.wait_recv()

        def total(k, part, b, i):
            if k == 2:
                return ar[36][it, b, i:i + C, :]
            return ar[13 * k + 10][it, part, b * M + i:b * M + i + C, :]

        sums = jnp.zeros((C, H), F32)
        for b in range(2):
            for i in range(0, M, C):
                sums = sums + total(2, 0, b, i)
        reg_probe = DAMPING * (jnp.sum(sums) * (1.0 / (M * M))) + SMALL
        for b in range(2):
            for i in range(0, M, C):
                scale = 1.0 / (total(2, 0, b, i) + reg_probe)
                for k in range(2):
                    for part in range(2):
                        at = (part, k, slice(i, i + C), slice(b * H, b * H + H))
                        probe[at] += total(k, part, b, i) * scale

        for n in range(len(streams)):
            for phase in range(1, 7):
                for copy in phase_copies(it, n, phase):
                    copy.wait_send()
        for ch in range(2):
            for s in range(2):
                pl.when(not_bottom)(lambda: down(it, s, ch).wait_send())
                pl.when(not_top & more)(lambda: up(it + 1, s, ch).wait_send())
        return 0

    for ch in range(2):
        for q in range(4):
            pl.when(not_left)(lambda: to_left(obj, 0, ch, q).wait_send())
        for s in range(2):
            pl.when(not_bottom)(lambda: up(0, s, ch).wait_recv())
            pl.when(not_top)(lambda: up(0, s, ch).wait_send())

    zero_sums()
    take_all(0)
    lax.fori_loop(0, ITERS, iteration, 0)

    stores = []
    for ch in range(2):
        for b in range(4):
            store = pltpu.make_async_copy(
                obj.at[ch, b, pl.ds(M, T), :], obj_out.at[ch, :, pl.ds(b * H, H)], io_sem.at[ch, b]
            )
            store.start()
            stores.append(store)
    for store in stores:
        store.wait()


def shards(rows_n, cols_n, nz, ny, object_field, probe_modes, intensities, positions, counts):
    sizes = {"x": rows_n // 2, "y": ny, "z": nz}
    streams = (
        Stream(1024, ("x", "z", "y"), sizes),
        Stream(1024, ("x", "y", "z"), sizes),
        Stream(512, ("x", "z", "y"), sizes),
    )
    vm = lambda *shape: pltpu.VMEM(shape, F32)
    sem = lambda *shape: pltpu.SemaphoreType.DMA(shape)
    consts = [jnp.asarray(t) for t in tables()]
    scratch = [vm(2, M, M)] + [pltpu.VMEM(t.shape, t.dtype) for t in consts]
    scratch += [
        vm(2, 6, 1024, H),
        vm(2, 6, T, H),
        vm(6, T, H),
        vm(2, 3, 1024, H),
        vm(3, 1024, H),
        vm(2, M, H),
        vm(2, 2, M, M),
        vm(2, 2, M, M),
        pltpu.VMEM((2, 3 * M, 2 * M), BF16),
        vm(2, M, 2 * M),
        pltpu.VMEM((2, 2 * M, 3 * M), BF16),
        vm(2, 2 * M, M),
        vm(2, M, M),
        vm(2, 2, 2, M, H),
        vm(2, 2, 2, M, H),
        vm(ITERS, 2, 4, 2, H, H),
        vm(ITERS, 2, 4, 2, H, H),
        vm(ITERS, 2, 2, 2, M, H),
        vm(ITERS, 2, 2, 2, M, H),
        sem(10),
        sem(2, 4),
        sem(ITERS, 2, 2, 4),
        sem(ITERS, 2, 2, 4),
        sem(ITERS, 2, 2),
        sem(ITERS, 2, 2),
        sem(ITERS, 2, 2),
        sem(ITERS, 2, 2),
    ]
    for st in streams:
        scratch += st.scratch()
    smem = pl.BlockSpec(memory_space=pltpu.SMEM)
    vmem = pl.BlockSpec(memory_space=pltpu.VMEM)
    hbm = pl.BlockSpec(memory_space=pl.ANY)
    return pl.pallas_call(
        functools.partial(kernel, rows_n, cols_n, nz, ny, streams),
        out_shape=(
            jax.ShapeDtypeStruct((2, T, T), F32),
            jax.ShapeDtypeStruct((2, 2, M, M), F32),
        ),
        in_specs=[smem, smem, hbm, hbm, hbm] + [hbm] * len(consts),
        out_specs=(hbm, vmem),
        scratch_shapes=scratch,
        compiler_params=pltpu.CompilerParams(
            collective_id=0, has_side_effects=True, vmem_limit_bytes=62 * 1024 * 1024
        ),
        name="ptycho",
    )(positions.T, counts, object_field, probe_modes, intensities, *consts)


def solution(mesh):
    rows_n, cols_n = mesh.shape["row"], mesh.shape["col"]
    ny = math.isqrt(cols_n)
    nz = cols_n // ny
    placed = (P(None, "row", "col"), P(), P(("row", "col"), None, None), P(), P())
    return jax.shard_map(
        functools.partial(shards, rows_n, cols_n, nz, ny),
        mesh=mesh,
        in_specs=placed,
        out_specs=(P(None, "row", "col"), P()),
        check_vma=False,
    )
```

```python
import functools
import math

import jax
import jax.numpy as jnp
import ml_dtypes
import numpy as np
from jax import lax
from jax.experimental import pallas as pl
from jax.experimental.pallas import tpu as pltpu
from jax.sharding import PartitionSpec as P

ITERS = 3
M = 256
H = 128
T = 512
MODEL_FLOOR = 0.5
DAMPING = 0.2
SMALL = 1e-06
MESH = pl.DeviceIdType.MESH
F32 = jnp.float32
BF16 = jnp.bfloat16


def tables():
    k = np.arange(H)
    angle = 2.0 * np.pi * ((k[:, None] * k[None, :]) % H) / H
    c, s = np.cos(angle) / 16.0, np.sin(angle) / 16.0

    def three(matrix, axis):
        wide = matrix.astype(np.float32)
        hi = wide.astype(ml_dtypes.bfloat16)
        lo = (wide - hi.astype(np.float32)).astype(ml_dtypes.bfloat16)
        return np.concatenate([hi, hi, lo], axis=axis)

    left = np.block([[c, s], [-s, c]])
    left_back = np.block([[c, -s], [s, c]])
    turn = 2.0 * np.pi * k / M
    rows = np.stack([np.cos(turn), np.sin(turn)])[:, :, None] * np.ones((1, 1, H))
    cols = rows.transpose(0, 2, 1)[:, :16]
    order = np.concatenate([np.arange(0, M, 2), np.arange(1, M, 2)])
    pick = np.zeros((M, M), np.float32)
    pick[np.arange(M), order] = 1.0
    return (
        three(left, 1),
        three(left_back, 1),
        three(left.T, 0),
        three(left_back.T, 0),
        rows.astype(np.float32),
        cols.astype(np.float32),
        pick.astype(ml_dtypes.bfloat16),
        np.ascontiguousarray(pick.T).astype(ml_dtypes.bfloat16),
    )


def dot(a, b):
    return jnp.dot(a, b, preferred_element_type=F32)


def cat(parts, axis):
    return jnp.concatenate(parts, axis=axis)


def split(x):
    hi = x.astype(BF16)
    lo = (x - hi.astype(F32)).astype(BF16)
    return hi, lo


def store_parts(ref, k, row, lane, axis, x):
    hi, lo = split(x)
    for n, part in enumerate((hi, lo, hi)):
        r, c = (row + n * M, lane) if axis == 0 else (row, lane + n * M)
        ref[k, r:r + 16, c:c + H] = part


class Stream:
    def __init__(self, rows, axes, sizes):
        self.half = rows // 2
        self.axes = axes
        self.n = [sizes[a] for a in axes]
        self.r1 = self.half // self.n[0]
        self.r2 = self.r1 // self.n[1]

    def scratch(self):
        vm = lambda *shape: pltpu.VMEM(shape, F32)
        n1, n2, n3 = self.n
        return [
            vm(2, self.half, H),
            vm(ITERS, self.half, H),
            vm(self.half, H),
            vm(ITERS, n1, self.r1, H),
            vm(self.r1, H),
            vm(ITERS, n2, self.r2, H),
            vm(self.r2, H),
            vm(ITERS, n3, self.r2, H),
            vm(ITERS, self.r1, H),
            vm(ITERS, self.half, H),
            vm(ITERS, 2, self.half, H),
            pltpu.SemaphoreType.DMA((ITERS, 7, 4)),
            pltpu.SemaphoreType.DMA((ITERS, 7, 4)),
        ]


def kernel(
    rows_n, cols_n, nz, ny, streams,
    pos, counts, obj_in, probe_in, meas_in, wl_in, wlb_in, wr_in, wrb_in, twr_in, twc_in, pick_in,
    pick_t_in, obj_out, probe,
    meas, wl, wlb, wr, wrb, twr, twc, pick, pick_t,
    obj, acc, den, zbuf, cbuf, power, patch, exits, lop, lout, rop, rout, root, upd, out_up,
    hr, hl, vu, vh,
    load_sem, io_sem, hs, hrs, vs, vrs, us, urs, *ar,
):
    nx = rows_n // 2
    row, col = lax.axis_index("row"), lax.axis_index("col")
    core, xi = lax.rem(row, 2), lax.div(row, 2)
    yi, zi = lax.rem(col, ny), lax.div(col, ny)
    me = {"x": xi, "y": yi, "z": zi}
    size = {"x": nx, "y": ny, "z": nz}

    def device(axis, j):
        if axis == "x":
            return (j * 2 + core, col)
        if axis == "y":
            return (row, zi * ny + j)
        return (row, j * ny + yi)

    partner = (row + 1 - 2 * core, col)
    not_left, not_right = col > 0, col < cols_n - 1
    not_top, not_bottom = row > 0, row < rows_n - 1

    loads = []
    for ch in range(2):
        for b in range(4):
            load = pltpu.make_async_copy(
                obj_in.at[ch, :, pl.ds(b * H, H)], obj.at[ch, b, pl.ds(M, T), :], io_sem.at[ch, b]
            )
            load.start()
            loads.append(load)
    later = []
    for i, (src, dst) in enumerate(
        (
            (meas_in, meas), (pick_in, pick), (pick_t_in, pick_t), (probe_in, probe), (wl_in, wl),
            (wlb_in, wlb), (wr_in, wr), (wrb_in, wrb), (twr_in, twr), (twc_in, twc),
        )
    ):
        load = pltpu.make_async_copy(src, dst, load_sem.at[i])
        load.start()
        later.append(load)

    barrier = pltpu.get_barrier_semaphore()

    def greet(who):
        pl.semaphore_signal(barrier, inc=1, device_id=who, device_id_type=MESH)

    greet(partner)
    peers = 1
    for axis in ("z", "y", "x"):
        for d in range(1, size[axis]):
            greet(device(axis, lax.rem(me[axis] + d, size[axis])))
            peers += 1
    pl.when(not_left)(lambda: greet((row, col - 1)))
    pl.when(not_right)(lambda: greet((row, col + 1)))
    pl.when(not_top)(lambda: greet((row - 1, col)))
    pl.when(not_bottom)(lambda: greet((row + 1, col)))

    zbuf[...] = jnp.zeros_like(zbuf)
    cbuf[...] = jnp.zeros_like(cbuf)

    @pl.when(jnp.logical_not(not_left))
    def _():
        hl[...] = jnp.zeros_like(hl)

    @pl.when(jnp.logical_not(not_right))
    def _():
        hr[...] = jnp.zeros_like(hr)

    @pl.when(jnp.logical_not(not_top))
    def _():
        vu[...] = jnp.zeros_like(vu)

    @pl.when(jnp.logical_not(not_bottom))
    def _():
        vh[...] = jnp.zeros_like(vh)

    for load in loads:
        load.wait()
    pl.semaphore_wait(
        barrier,
        peers
        + not_left.astype(jnp.int32) + not_right.astype(jnp.int32)
        + not_top.astype(jnp.int32) + not_bottom.astype(jnp.int32),
    )

    def remote(src, dst, send, recv, who):
        return pltpu.make_async_remote_copy(
            src_ref=src, dst_ref=dst, send_sem=send, recv_sem=recv, device_id=who, device_id_type=MESH
        )

    def to_left(src, turn, ch, q):
        base = M if src is obj else 0
        return remote(
            src.at[ch, pl.ds(0, 2), pl.ds(base + q * H, H), :], hr.at[turn, ch, q],
            hs.at[turn, 0, ch, q], hrs.at[turn, 0, ch, q], (row, col - 1),
        )

    def to_right(turn, ch, q):
        return remote(
            acc.at[ch, pl.ds(4, 2), pl.ds(q * H, H), :], hl.at[turn, ch, q],
            hs.at[turn, 1, ch, q], hrs.at[turn, 1, ch, q], (row, col + 1),
        )

    def down(it, s, ch):
        return remote(
            upd.at[s, ch], vu.at[it, s, ch], us.at[it, s, ch], urs.at[it, s, ch], (row + 1, col)
        )

    def up(turn, s, ch):
        return remote(
            out_up.at[s, ch], vh.at[turn, s, ch], vs.at[turn, s, ch], vrs.at[turn, s, ch],
            (row - 1, col),
        )

    C = 64
    lane = lax.broadcasted_iota(jnp.int32, (C, H), 1)
    line = lax.broadcasted_iota(jnp.int32, (C, H), 0)

    def place_of(dr, dc, s):
        r, c = row + dr, col + dc
        there = (r >= 0) & (r < rows_n) & (c >= 0) & (c < cols_n)
        r, c = jnp.clip(r, 0, rows_n - 1), jnp.clip(c, 0, cols_n - 1)
        dev = r * cols_n + c
        y = jnp.clip(pos[0, dev * 2 + s] - r * T, 0, T - 1)
        x = jnp.clip(pos[1, dev * 2 + s] - c * T, 0, T - 1)
        live = jnp.where(there & (s < counts[dev]), 1.0, 0.0).astype(F32)
        return y, x, live

    def extract(ch, start, x, store):
        q, r = lax.div(x, H), lax.rem(x, H)
        back = lax.rem(H - r, H)
        keep = lane < H - r
        for i in range(0, M, C):
            b = [pltpu.roll(obj[ch, q + j, pl.ds(start + i, C), :], back, 1) for j in range(3)]
            store(i, jnp.where(keep, b[0], b[1]), jnp.where(keep, b[1], b[2]))

    def spread(z, load, x):
        r = lax.rem(x, H)
        keep = lane >= r
        for i in range(0, M, C):
            u0, u1 = load(i)
            a, b = pltpu.roll(u0, r, 1), pltpu.roll(u1, r, 1)
            z[0, T + i:T + i + C, :] = jnp.where(keep, a, 0.0)
            z[1, T + i:T + i + C, :] = jnp.where(keep, b, a)
            z[2, T + i:T + i + C, :] = jnp.where(keep, 0.0, b)

    def add_placed(z, dst, blocks, dr, dc, y, x, weight):
        q = lax.div(x, H) + 4 * dc
        length = T if dr == 0 else M
        start = T - y - dr * T
        if dr != 0:
            start = jnp.minimum(start, 3 * M)
        for b in blocks:
            j = b - q
            inside = jnp.where((j >= 0) & (j <= 2), weight, 0.0).astype(F32)
            near = jnp.clip(j, 0, 2)
            for i in range(0, length, C):
                dst[b, i:i + C, :] += z[near, pl.ds(start + i, C), :] * inside

    def send_up(turn, ch):
        for s in range(2):
            y, x, _ = place_of(-1, 0, s)

            def store(i, b0, b1, s=s):
                out_up[s, ch, 0, i:i + C, :] = b0
                out_up[s, ch, 1, i:i + C, :] = b1

            extract(ch, jnp.maximum(y - T, -M) + M, x, store)
            pl.when(not_top)(lambda: up(turn, s, ch).start())

    first = [(ch, q) for half in range(2) for ch in range(2) for q in (2 * half, 2 * half + 1)]

    def first_piece(n):
        pl.when(not_left)(lambda: to_left(obj, 0, *first[n]).start())

    first_piece(0)
    first_piece(1)

    for load in later:
        load.wait()

    for s in range(2):
        value = meas[s]
        for step in range(2):
            h = value.astype(BF16)
            rest = value - h.astype(F32)
            m = rest.astype(BF16)
            low = (rest - m.astype(F32)).astype(BF16)
            if step == 0:
                value = (dot(pick[...], h) + dot(pick[...], m)) + dot(pick[...], low)
            else:
                value = (dot(h, pick_t[...]) + dot(m, pick_t[...])) + dot(low, pick_t[...])
        root[s] = jnp.sqrt(value)

    for n, (ch, q) in enumerate(first):
        with jax.named_scope("first_piece"):
            pl.when(not_right)(lambda: to_left(obj, 0, ch, q).wait_recv())
        if n + 2 < len(first):
            first_piece(n + 2)
        for b in range(2):
            for i in range(0, H, C):
                obj[ch, 4 + b, M + q * H + i:M + q * H + i + C, :] = hr[0, ch, q, b, i:i + C, :]
        if q == 1:
            send_up(0, ch)

    def take(it, s):
        y, x, live = place_of(0, 0, s)

        def store(i, b0, b1, ch):
            own = line + i < T - y
            parts = (b0, b1)
            for b in range(2):
                value = jnp.where(own, parts[b], vh[it, s, ch, b, i:i + C, :])
                patch[s, ch, i:i + C, b * H:(b + 1) * H] = value
                sum_ref(2, 0, b)[i:i + C, :] += value * value * live

        for ch in range(2):
            extract(ch, M + y, x, functools.partial(store, ch=ch))

    def slot(it, s):
        _, _, live = place_of(0, 0, s)
        cc, sc = twc[0], twc[1]
        lanes = (slice(0, H), slice(H, M))
        for k in range(2):
            for i in range(0, H, 16):
                cr, sr = twr[0, i:i + 16, :], twr[1, i:i + 16, :]
                for b in range(2):
                    er, ei = [], []
                    for t in (i, i + H):
                        at = (slice(t, t + 16), lanes[b])
                        pr, pi = patch[(s, 0) + at], patch[(s, 1) + at]
                        qr, qi = probe[(0, k) + at], probe[(1, k) + at]
                        er.append(qr * pr - qi * pi)
                        ei.append(qr * pi + qi * pr)
                        exits[(k, 0) + at] = er[-1]
                        exits[(k, 1) + at] = ei[-1]
                    dr, di = er[0] - er[1], ei[0] - ei[1]
                    store_parts(lop, k, i, b * H, 0, er[0] + er[1])
                    store_parts(lop, k, i + H, b * H, 0, ei[0] + ei[1])
                    store_parts(lop, k, i, M + b * H, 0, dr * cr + di * sr)
                    store_parts(lop, k, i + H, M + b * H, 0, di * cr - dr * sr)
            lout[k] = dot(wl[...], lop[k])
        for k in range(2):
            for i in range(0, M, 16):
                j, c = i % H, (i // H) * M
                lr = [lout[k, j:j + 16, c + b * H:c + b * H + H] for b in range(2)]
                li = [lout[k, j + H:j + H + 16, c + b * H:c + b * H + H] for b in range(2)]
                dr, di = lr[0] - lr[1], li[0] - li[1]
                store_parts(rop, k, i, 0, 1, lr[0] + lr[1])
                store_parts(rop, k, i, H, 1, li[0] + li[1])
                store_parts(rop, k, i + M, 0, 1, dr * cc + di * sc)
                store_parts(rop, k, i + M, H, 1, di * cc - dr * sc)
            rout[k] = dot(rop[k], wr[...])
        for i in range(0, 2 * M, 16):
            f = [[rout[k, i:i + 16, lanes[b]] for b in range(2)] for k in range(2)]
            model = (f[0][0] * f[0][0] + f[0][1] * f[0][1]) + (f[1][0] * f[1][0] + f[1][1] * f[1][1])
            scale = root[s, i % M:i % M + 16, lanes[i // M]]
            scale = scale * lax.rsqrt(jnp.maximum(model, MODEL_FLOOR))
            for k in range(2):
                for b in range(2):
                    store_parts(rop, k, i, b * H, 1, f[k][b] * scale)
        for k in range(2):
            rout[k] = dot(rop[k], wrb[...])
        for k in range(2):
            for i in range(0, M, 16):
                er, ei = rout[k, i:i + 16, lanes[0]], rout[k, i:i + 16, lanes[1]]
                dr, di = rout[k, i + M:i + M + 16, lanes[0]], rout[k, i + M:i + M + 16, lanes[1]]
                tr, ti = dr * cc - di * sc, di * cc + dr * sc
                j, c = i % H, (i // H) * M
                store_parts(lop, k, j, c, 0, er + tr)
                store_parts(lop, k, j, c + H, 0, er - tr)
                store_parts(lop, k, j + H, c, 0, ei + ti)
                store_parts(lop, k, j + H, c + H, 0, ei - ti)
            lout[k] = dot(wlb[...], lop[k])
        for i in range(0, H, 16):
            cr, sr = twr[0, i:i + 16, :], twr[1, i:i + 16, :]
            for b in range(2):
                u = [[None, None], [None, None]]
                for k in range(2):
                    c = b * H
                    er, ei = lout[k, i:i + 16, c:c + H], lout[k, i + H:i + H + 16, c:c + H]
                    dr = lout[k, i:i + 16, M + c:M + c + H]
                    di = lout[k, i + H:i + H + 16, M + c:M + c + H]
                    tr, ti = dr * cr - di * sr, di * cr + dr * sr
                    for n, (gr, gi) in enumerate(((er + tr, ei + ti), (er - tr, ei - ti))):
                        t = i + n * H
                        at = (slice(t, t + 16), lanes[b])
                        gr = (gr - exits[(k, 0) + at]) * live
                        gi = (gi - exits[(k, 1) + at]) * live
                        qr, qi = probe[(0, k) + at], probe[(1, k) + at]
                        pr, pi = patch[(s, 0) + at], patch[(s, 1) + at]
                        ur, ui = qr * gr + qi * gi, qr * gi - qi * gr
                        if k == 0:
                            u[n] = [ur, ui]
                        else:
                            upd[s, 0, b, t:t + 16, :] = u[n][0] + ur
                            upd[s, 1, b, t:t + 16, :] = u[n][1] + ui
                        sum_ref(k, 0, b)[t:t + 16, :] += pr * gr + pi * gi
                        sum_ref(k, 1, b)[t:t + 16, :] += pr * gi - pi * gr
        for ch in range(2):
            pl.when(not_bottom)(lambda: down(it, s, ch).start())

    def place(ch, dr, s, src):
        y, x, _ = place_of(dr, 0, s)
        spread(zbuf.at[ch], lambda i: (src[0, i:i + C, :], src[1, i:i + C, :]), x)
        add_placed(zbuf.at[ch], acc.at[ch], range(6), dr, 0, y, x, 1.0)

    def sum_ref(k, part, b):
        if k == 2:
            return ar[26].at[b]
        return ar[13 * k].at[part, pl.ds(b * M, M), :]

    def group(it, n, phase, axis, src, dst):
        ssem, rsem = ar[13 * n + 11], ar[13 * n + 12]
        out = []
        for d in range(1, size[axis]):
            j = lax.rem(me[axis] + d, size[axis])
            out.append(
                remote(src(j), dst, ssem.at[it, phase, d], rsem.at[it, phase, d], device(axis, j))
            )
        return out

    def phase_copies(it, n, phase):
        st = streams[n]
        own, cin, m0, r1, m1, r2, m2, r3, g2, g1, gc, ssem, rsem = ar[13 * n:13 * n + 13]
        a, b, c = st.axes
        R1, R2 = st.r1, st.r2
        rows_of = lambda j, r: pl.ds(pl.multiple_of(j * r, 8), r)
        if phase == 0:
            return [remote(own.at[1 - core], cin.at[it], ssem.at[it, 0, 0], rsem.at[it, 0, 0], partner)]
        if phase == 1:
            return group(it, n, 1, a, lambda j: m0.at[rows_of(j, R1), :], r1.at[it, me[a]])
        if phase == 2:
            return group(it, n, 2, b, lambda j: m1.at[rows_of(j, R2), :], r2.at[it, me[b]])
        if phase == 3:
            return group(it, n, 3, c, lambda j: m2, r3.at[it, me[c]])
        if phase == 4:
            part = g2.at[it, rows_of(me[b], R2), :]
            return group(it, n, 4, b, lambda j: part, part)
        if phase == 5:
            part = g1.at[it, rows_of(me[a], R1), :]
            return group(it, n, 5, a, lambda j: part, part)
        part = gc.at[it, core]
        return [remote(part, part, ssem.at[it, 6, 0], rsem.at[it, 6, 0], partner)]

    def ar_start(it, which):
        for n in which:
            for copy in phase_copies(it, n, 0):
                copy.start()

    def ar_step(it, which, phase):
        for n in which:
            st = streams[n]
            own, cin, m0, r1, m1, r2, m2, r3, g2, g1, gc, ssem, rsem = ar[13 * n:13 * n + 13]
            a, b, c = st.axes
            rows_of = lambda j, r: pl.ds(pl.multiple_of(j * r, 8), r)
            for copy in phase_copies(it, n, phase):
                copy.wait_recv()
            if phase == 0:
                for i in range(0, st.half, C):
                    m0[i:i + C, :] = own[core, i:i + C, :] + cin[it, i:i + C, :]
                r1[it, me[a]] = m0[rows_of(me[a], st.r1), :]
            elif phase == 1:
                m1[...] = functools.reduce(lambda p, q: p + q, [r1[it, j] for j in range(st.n[0])])
                r2[it, me[b]] = m1[rows_of(me[b], st.r2), :]
            elif phase == 2:
                m2[...] = functools.reduce(lambda p, q: p + q, [r2[it, j] for j in range(st.n[1])])
                r3[it, me[c]] = m2[...]
            elif phase == 3:
                g2[it, rows_of(me[b], st.r2), :] = functools.reduce(
                    lambda p, q: p + q, [r3[it, j] for j in range(st.n[2])]
                )
            elif phase == 4:
                g1[it, rows_of(me[a], st.r1), :] = g2[it]
            elif phase == 5:
                gc[it, core] = g1[it]
            if phase < 6:
                for copy in phase_copies(it, n, phase + 1):
                    copy.start()

    mode_sums, power_sum = (0, 1), (2,)

    def zero_sums():
        acc[...] = jnp.zeros_like(acc)
        for n in range(3):
            ar[13 * n][...] = jnp.zeros_like(ar[13 * n])

    def take_all(it):
        for s in range(2):
            take(it, s)
        ar_start(it, power_sum)

    def iteration(it, _):
        more = it < ITERS - 1
        send_left = not_left & more
        get_right = not_right & more
        scope = jax.named_scope

        def one(s, carry):
            slot(it, s)

            @pl.when(s == 0)
            def _():
                ar_step(it, power_sum, 0)

            return carry

        with scope("slots"):
            lax.fori_loop(0, 2, one, 0)
        ar_start(it, mode_sums)

        def send(ch, q):
            pl.when(not_right & (core == 0))(lambda: to_right(it, ch, q).start())
            pl.when(send_left)(lambda: to_left(acc, it + 1, ch, q).start())
            pl.when(not_right & (core == 1))(lambda: to_right(it, ch, q).start())

        def arrive(ch, q):
            pl.when(not_left)(lambda: to_right(it, ch, q).wait_recv())
            pl.when(get_right)(lambda: to_left(acc, it + 1, ch, q).wait_recv())

        def update(ch, q):
            for i in range(q * H, q * H + H, C):
                rows, there, j = slice(i, i + C), slice(M + i, M + i + C), i - q * H
                for b in range(4):
                    step = acc[ch, b, rows, :]
                    if b < 2:
                        step = step + hl[it, ch, q, b, j:j + C, :]
                    obj[ch, b, there, :] += step * den[b, rows, :]

            @pl.when(get_right)
            def _():
                for i in range(q * H, q * H + H, C):
                    rows, there, j = slice(i, i + C), slice(M + i, M + i + C), i - q * H
                    for b in range(2):
                        step = acc[ch, 4 + b, rows, :] + hr[it + 1, ch, q, b, j:j + C, :]
                        obj[ch, 4 + b, there, :] += step * den[4 + b, rows, :]

        def clear(it):
            for ch in range(2):
                for q in range(4):
                    pl.when(not_right)(lambda: to_right(it, ch, q).wait_send())
                    pl.when(send_left)(lambda: to_left(acc, it + 1, ch, q).wait_send())
            for n in range(len(streams)):
                for copy in phase_copies(it, n, 0):
                    copy.wait_send()
            zero_sums()

        def below(s, ch):
            pl.when(not_top)(lambda: down(it, s, ch).wait_recv())
            place(ch, -1, s, vu.at[it, s, ch])

        for ch in range(2):
            for s in range(2):
                place(ch, 0, s, upd.at[s, ch])
            if ch == 0:
                send(0, 2)
                send(0, 3)
        with scope("core_sums"):
            ar_step(it, power_sum, 1)
            ar_step(it, mode_sums, 0)
        with scope("from_above"):
            for q in range(2):
                if q == 0:
                    below(0, 0)
                    below(1, 0)
                arrive(0, 2 + q)
                send(0, q)
            below(0, 1)
            below(1, 1)
        send(1, 0)
        ar_step(it, power_sum, 2)

        with scope("coverage"):
            power_all = jnp.zeros((C, H), F32)
            for b in range(2):
                for i in range(0, M, C):
                    at = (slice(i, i + C), slice(b * H, b * H + H))
                    square = (
                        probe[(0, 0) + at] ** 2 + probe[(1, 0) + at] ** 2
                        + probe[(0, 1) + at] ** 2 + probe[(1, 1) + at] ** 2
                    )
                    power[b, i:i + C, :] = square
                    power_all = power_all + square
            reg_object = DAMPING * (jnp.sum(power_all) * (1.0 / (M * M))) + SMALL
            den[...] = jnp.zeros_like(den)
            for dr in (0, -1):
                for dc, blocks in ((0, range(6)), (-1, range(2)), (1, range(4, 6))):

                    def cover(s, carry, dr=dr, dc=dc, blocks=blocks):
                        y, x, live = place_of(dr, dc, s)
                        spread(cbuf, lambda i: (power[0, i:i + C, :], power[1, i:i + C, :]), x)
                        add_placed(cbuf, den, blocks, dr, dc, y, x, live)
                        return carry

                    lax.fori_loop(0, 2, cover, 0)
            for b in range(6):
                for i in range(0, T, C):
                    den[b, i:i + C, :] = 1.0 / (den[b, i:i + C, :] + reg_object)

        with scope("piece_00"):
            arrive(0, 0)
        send(1, 1)
        update(0, 0)
        with scope("first_split"):
            ar_step(it, mode_sums, 1)
        with scope("piece_01"):
            arrive(0, 1)
        send(1, 2)
        update(0, 1)
        pl.when(more)(lambda: send_up(it + 1, 0))
        ar_step(it, power_sum, 3)
        with scope("second_split"):
            ar_step(it, mode_sums, 2)
        with scope("piece_10"):
            arrive(1, 0)
        send(1, 3)
        update(1, 0)
        with scope("exchange"):
            ar_step(it, mode_sums, 3)
        with scope("piece_11"):
            arrive(1, 1)
        update(1, 1)
        pl.when(more)(lambda: send_up(it + 1, 1))
        update(0, 2)
        update(0, 3)
        ar_step(it, power_sum, 4)
        with scope("first_gather"):
            ar_step(it, mode_sums, 4)
        with scope("piece_12"):
            arrive(1, 2)
        update(1, 2)
        ar_step(it, power_sum, 5)
        with scope("piece_13"):
            arrive(1, 3)
        update(1, 3)
        clear(it)

        @pl.when(more)
        def _():
            with scope("from_below"):
                for ch in range(2):
                    for s in range(2):
                        pl.when(not_bottom)(lambda: up(it + 1, s, ch).wait_recv())
            take_all(it + 1)

        with scope("second_gather"):
            ar_step(it, mode_sums, 5)
        with scope("core_gather"):
            for n in range(len(streams)):
                for copy in phase_copies(it, n, 6):
                    copy.wait_recv()

        def total(k, part, b, i):
            if k == 2:
                return ar[36][it, b, i:i + C, :]
            return ar[13 * k + 10][it, part, b * M + i:b * M + i + C, :]

        sums = jnp.zeros((C, H), F32)
        for b in range(2):
            for i in range(0, M, C):
                sums = sums + total(2, 0, b, i)
        reg_probe = DAMPING * (jnp.sum(sums) * (1.0 / (M * M))) + SMALL
        for b in range(2):
            for i in range(0, M, C):
                scale = 1.0 / (total(2, 0, b, i) + reg_probe)
                for k in range(2):
                    for part in range(2):
                        at = (part, k, slice(i, i + C), slice(b * H, b * H + H))
                        probe[at] += total(k, part, b, i) * scale

        for n in range(len(streams)):
            for phase in range(1, 7):
                for copy in phase_copies(it, n, phase):
                    copy.wait_send()
        for ch in range(2):
            for s in range(2):
                pl.when(not_bottom)(lambda: down(it, s, ch).wait_send())
                pl.when(not_top & more)(lambda: up(it + 1, s, ch).wait_send())
        return 0

    for ch in range(2):
        for q in range(4):
            pl.when(not_left)(lambda: to_left(obj, 0, ch, q).wait_send())
        for s in range(2):
            pl.when(not_bottom)(lambda: up(0, s, ch).wait_recv())
            pl.when(not_top)(lambda: up(0, s, ch).wait_send())

    zero_sums()
    take_all(0)
    lax.fori_loop(0, ITERS, iteration, 0)

    stores = []
    for ch in range(2):
        for b in range(4):
            store = pltpu.make_async_copy(
                obj.at[ch, b, pl.ds(M, T), :], obj_out.at[ch, :, pl.ds(b * H, H)], io_sem.at[ch, b]
            )
            store.start()
            stores.append(store)
    for store in stores:
        store.wait()


def shards(rows_n, cols_n, nz, ny, object_field, probe_modes, intensities, positions, counts):
    sizes = {"x": rows_n // 2, "y": ny, "z": nz}
    streams = (
        Stream(1024, ("x", "z", "y"), sizes),
        Stream(1024, ("x", "y", "z"), sizes),
        Stream(512, ("x", "z", "y"), sizes),
    )
    vm = lambda *shape: pltpu.VMEM(shape, F32)
    sem = lambda *shape: pltpu.SemaphoreType.DMA(shape)
    consts = [jnp.asarray(t) for t in tables()]
    scratch = [vm(2, M, M)] + [pltpu.VMEM(t.shape, t.dtype) for t in consts]
    scratch += [
        vm(2, 6, 1024, H),
        vm(2, 6, T, H),
        vm(6, T, H),
        vm(2, 3, 1024, H),
        vm(3, 1024, H),
        vm(2, M, H),
        vm(2, 2, M, M),
        vm(2, 2, M, M),
        pltpu.VMEM((2, 3 * M, 2 * M), BF16),
        vm(2, M, 2 * M),
        pltpu.VMEM((2, 2 * M, 3 * M), BF16),
        vm(2, 2 * M, M),
        vm(2, M, M),
        vm(2, 2, 2, M, H),
        vm(2, 2, 2, M, H),
        vm(ITERS, 2, 4, 2, H, H),
        vm(ITERS, 2, 4, 2, H, H),
        vm(ITERS, 2, 2, 2, M, H),
        vm(ITERS, 2, 2, 2, M, H),
        sem(10),
        sem(2, 4),
        sem(ITERS, 2, 2, 4),
        sem(ITERS, 2, 2, 4),
        sem(ITERS, 2, 2),
        sem(ITERS, 2, 2),
        sem(ITERS, 2, 2),
        sem(ITERS, 2, 2),
    ]
    for st in streams:
        scratch += st.scratch()
    smem = pl.BlockSpec(memory_space=pltpu.SMEM)
    vmem = pl.BlockSpec(memory_space=pltpu.VMEM)
    hbm = pl.BlockSpec(memory_space=pl.ANY)
    return pl.pallas_call(
        functools.partial(kernel, rows_n, cols_n, nz, ny, streams),
        out_shape=(
            jax.ShapeDtypeStruct((2, T, T), F32),
            jax.ShapeDtypeStruct((2, 2, M, M), F32),
        ),
        in_specs=[smem, smem, hbm, hbm, hbm] + [hbm] * len(consts),
        out_specs=(hbm, vmem),
        scratch_shapes=scratch,
        compiler_params=pltpu.CompilerParams(
            collective_id=0, has_side_effects=True, vmem_limit_bytes=62 * 1024 * 1024
        ),
        name="ptycho",
    )(positions.T, counts, object_field, probe_modes, intensities, *consts)


def solution(mesh):
    rows_n, cols_n = mesh.shape["row"], mesh.shape["col"]
    ny = math.isqrt(cols_n)
    nz = cols_n // ny
    placed = (P(None, "row", "col"), P(), P(("row", "col"), None, None), P(), P())
    return jax.shard_map(
        functools.partial(shards, rows_n, cols_n, nz, ny),
        mesh=mesh,
        in_specs=placed,
        out_specs=(P(None, "row", "col"), P()),
        check_vma=False,
    )
```
